32 devices in a mesh: pole: 2 (over x), row: 16 (over z, y, core).
Axes of the slice: x: 2, y: 2, z: 4, core: 2. Of those that a mesh axis runs over, the one named last changes fastest.
Arguments:
- ainv_root: float32 [4, 512, 512], P('pole', 'row'), parts along dimension 0, as said below
- pattern: int32 [4, 4], replicated, may hold values 0 or 1
- panel_top: float32 [4, 2048, 128], P('pole', 'row'), parts along dimension 0, may hold values from -0.25 to 0.25
- inv_top: float32 [4, 512, 128], P('pole', 'row'), parts along dimension 0, may hold values from -6 to 6
- panel_mid: float32 [4, 4096, 128], P('pole', 'row'), parts along dimension 0, may hold values from -0.25 to 0.25
- link_mid: float32 [4, 1024, 128], P('pole', 'row'), parts along dimension 0, may hold values from -0.5 to 0.5
- inv_mid: float32 [4, 1024, 128], P('pole', 'row'), parts along dimension 0, may hold values from -6 to 6
- panel_leaf: float32 [4, 24576, 128], P('pole', 'row'), parts along dimension 0, may hold values from -0.25 to 0.25
- link_leaf_mid: float32 [4, 6144, 128], P('pole', 'row'), parts along dimension 0, may hold values from -0.5 to 0.5
- link_leaf_top: float32 [4, 6144, 128], P('pole', 'row'), parts along dimension 0, may hold values from -0.5 to 0.5
- inv_leaf: float32 [4, 6144, 128], P('pole', 'row'), parts along dimension 0, may hold values from -6 to 6
Outputs:
- col_top: float32 [4, 2048, 128], P('pole', 'row'), parts along dimension 0
- diag_top: float32 [4, 512, 128], P('pole', 'row'), parts along dimension 0
- col_mid: float32 [4, 4096, 128], P('pole', 'row'), parts along dimension 0
- cross_mid: float32 [4, 1024, 128], P('pole', 'row'), parts along dimension 0
- diag_mid: float32 [4, 1024, 128], P('pole', 'row'), parts along dimension 0
- col_leaf: float32 [4, 24576, 128], P('pole', 'row'), parts along dimension 0
- cross_leaf_mid: float32 [4, 6144, 128], P('pole', 'row'), parts along dimension 0
- cross_leaf_top: float32 [4, 6144, 128], P('pole', 'row'), parts along dimension 0
- diag_leaf: float32 [4, 6144, 128], P('pole', 'row'), parts along dimension 0
The draws below stay inside these ranges and needn't reach their ends.
There are 2 independent parts, one for each index of `pole`. The reference program is written for one: setup_inputs(seed, part) draws one part's arguments, and reference() takes and returns one part's arrays. A program takes and returns all parts, laid end to end along the dimension named above; an argument that names none is the same for every part. Nothing has to cross between parts.
Inputs may be any that keep to these rules, and one draw needn't show every extreme that they name: ainv_root is complex symmetric: ainv_root[c, i, k] equals ainv_root[c, k, i].
All inputs are finite; a program needn't handle non-finite values.
Results may differ from the reference program's by a relative error of at most 0.00009.
Values sent between devices are 32-bit elements; how exact they have to be, the bound alone decides.
No kernel may reach another device: no remote copies, remote signals or barrier semaphores. Data moves between devices by JAX's collectives and lax.ppermute only.
A program may use at most 64 MiB of HBM per device.

```python
import jax
import jax.numpy as jnp
from jax import lax

B = 128
NR = 4
LEAF = 3
NRB = 512
N_TOP = 4
N_MID = 8
N_LEAF = 48


def draw_ainv_root(key, part):
    key = jax.random.fold_in(key, 11)
    base = jax.random.normal(key, (2, NR * B, NR * B), jnp.float32)
    return (base + jnp.swapaxes(base, 1, 2)) * 0.7071


def place_ends(entries, stream_key, least, high):
    longest = entries.shape.index(max(entries.shape))
    spots = []
    for shift in (0, 1):
        where = [jax.random.randint(jax.random.fold_in(stream_key, axis), (), 0, length) for axis, length in enumerate(entries.shape)]
        where[longest] = (where[longest] + shift) % entries.shape[longest]
        spots.append(tuple(where))
    return entries.at[spots[0]].set(least).at[spots[1]].set(high)


def block_levels(rng, shape, cuts, low, top_value):
    factor_of = 1.0
    for position, blocks in cuts:
        draws = jax.random.uniform(jax.random.fold_in(jax.random.fold_in(rng, 6), position), (blocks,), jnp.float32, low / len(cuts), top_value / len(cuts))
        factor_of = factor_of * jnp.repeat(jnp.exp(draws), shape[position] // blocks).reshape((-1,) + (1,) * (len(shape) - 1 - position))
    return factor_of


def normal_values(own_key, shape, spread, most, shards=(), dtype=jnp.bfloat16):
    array = spread * jax.random.normal(own_key, shape, jnp.float32)
    if shards:
        array = array * block_levels(own_key, shape, shards, -0.22, 0.18)
    return jnp.clip(array, -most, most).astype(dtype)


def setup_inputs(seed: int = 0, part: int = 0) -> dict:
    arg_keys = jax.random.split(jax.random.key(seed), 12)
    own_keys = jax.random.split(jax.random.fold_in(arg_keys[11], part), 12)
    ainv_root = draw_ainv_root(jax.random.fold_in(jax.random.fold_in(arg_keys[11], part), 71), part)
    pattern = place_ends((jax.random.randint(arg_keys[1], (N_TOP, NR), 0, 2) < 1).astype(jnp.int32), jax.random.fold_in(arg_keys[1], 1), 0, 1)
    panel_top = normal_values(own_keys[2], (2, N_TOP * NRB, B), NRB ** -0.5, 0.25, ((1, 16),), jnp.float32)
    inv_top = normal_values(own_keys[3], (2, N_TOP * B, B), 1.0, 6.0, ((1, 16),), jnp.float32)
    panel_mid = normal_values(own_keys[4], (2, N_MID * NRB, B), NRB ** -0.5, 0.25, ((1, 16),), jnp.float32)
    link_mid = normal_values(own_keys[5], (2, N_MID * B, B), B ** -0.5, 0.5, ((1, 16),), jnp.float32)
    inv_mid = normal_values(own_keys[6], (2, N_MID * B, B), 1.0, 6.0, ((1, 16),), jnp.float32)
    panel_leaf = normal_values(own_keys[7], (2, N_LEAF * NRB, B), NRB ** -0.5, 0.25, ((1, 16),), jnp.float32)
    link_leaf_mid = normal_values(own_keys[8], (2, N_LEAF * B, B), B ** -0.5, 0.5, ((1, 16),), jnp.float32)
    link_leaf_top = normal_values(own_keys[9], (2, N_LEAF * B, B), B ** -0.5, 0.5, ((1, 16),), jnp.float32)
    inv_leaf = normal_values(own_keys[10], (2, N_LEAF * B, B), 1.0, 6.0, ((1, 16),), jnp.float32)
    return {"ainv_root": ainv_root, "pattern": pattern, "panel_top": panel_top, "inv_top": inv_top, "panel_mid": panel_mid, "link_mid": link_mid, "inv_mid": inv_mid, "panel_leaf": panel_leaf, "link_leaf_mid": link_leaf_mid, "link_leaf_top": link_leaf_top, "inv_leaf": inv_leaf}


HIGHEST_PRECISION = lax.Precision.HIGHEST


def pair_mult(left, right, form):
    def complex_term(first, second):
        return jnp.einsum(form, first, second, precision=HIGHEST_PRECISION, preferred_element_type=jnp.float32)
    real_part = complex_term(left[0], right[0]) - complex_term(left[1], right[1])
    imag_part = complex_term(left[0], right[1]) + complex_term(left[1], right[0])
    return jnp.stack([real_part, imag_part])


def reference(ainv_root, pattern, panel_top, inv_top, panel_mid, link_mid, inv_mid, panel_leaf, link_leaf_mid, link_leaf_top, inv_leaf):
    root_width = NR * B
    pattern_rows = jnp.repeat(pattern.astype(jnp.float32), B, axis=1)
    mask_top = pattern_rows[None, :, :, None]

    def root_times(columns):
        node_count = columns.shape[1]
        flat_cols = jnp.transpose(columns, (0, 2, 1, 3)).reshape(2, root_width, node_count * B)
        result = pair_mult(ainv_root, flat_cols, "ab,bc->ac").reshape(2, root_width, node_count, B)
        return jnp.transpose(result, (0, 2, 1, 3))

    top_masked = panel_top.reshape(2, N_TOP, root_width, B) * mask_top
    col_top = -(root_times(top_masked) * mask_top)
    diag_top = inv_top.reshape(2, N_TOP, B, B) - pair_mult(top_masked, col_top, "nba,nbc->nac")

    mask_mid = jnp.repeat(pattern_rows, 2, axis=0)[None, :, :, None]
    col_up = jnp.repeat(col_top, 2, axis=1)
    diag_up = jnp.repeat(diag_top, 2, axis=1)
    mid_link = link_mid.reshape(2, N_MID, B, B)
    mid_masked = panel_mid.reshape(2, N_MID, root_width, B) * mask_mid
    col_mid = -(pair_mult(col_up, mid_link, "nab,nbc->nac") + root_times(mid_masked) * mask_mid)
    cross_mid = -(pair_mult(diag_up, mid_link, "nab,nbc->nac") + pair_mult(col_up, mid_masked, "nba,nbc->nac"))
    diag_mid = inv_mid.reshape(2, N_MID, B, B) - pair_mult(mid_link, cross_mid, "nba,nbc->nac") - pair_mult(mid_masked, col_mid, "nba,nbc->nac")

    family = 2 * LEAF
    leaf_masked = panel_leaf.reshape(2, N_MID, family, root_width, B) * mask_mid[:, :, None]
    link_parent = link_leaf_mid.reshape(2, N_MID, family, B, B)
    link_grand = link_leaf_top.reshape(2, N_MID, family, B, B)
    leaf_inverse = inv_leaf.reshape(2, N_MID, family, B, B)

    def leaf_work(items):
        leaf_cols, parent_link, grand_link, own_inverse, mid_col, top_col, mid_cross, mid_diag, top_diag, row_mask = items
        flat_cols = jnp.transpose(leaf_cols, (0, 2, 1, 3)).reshape(2, root_width, family * B)
        product = pair_mult(ainv_root, flat_cols, "ab,bc->ac").reshape(2, root_width, family, B)
        product = jnp.transpose(product, (0, 2, 1, 3))
        col_out = -(pair_mult(mid_col, parent_link, "rb,lbc->lrc") + pair_mult(top_col, grand_link, "rb,lbc->lrc") + product * row_mask[:, None])
        cross_parent = -(pair_mult(mid_diag, parent_link, "ab,lbc->lac") + pair_mult(mid_cross, grand_link, "ba,lbc->lac") + pair_mult(mid_col, leaf_cols, "ra,lrc->lac"))
        cross_grand = -(pair_mult(mid_cross, parent_link, "ab,lbc->lac") + pair_mult(top_diag, grand_link, "ab,lbc->lac") + pair_mult(top_col, leaf_cols, "ra,lrc->lac"))
        diag_out = own_inverse - pair_mult(parent_link, cross_parent, "lba,lbc->lac") - pair_mult(grand_link, cross_grand, "lba,lbc->lac") - pair_mult(leaf_cols, col_out, "lra,lrc->lac")
        return col_out, cross_parent, cross_grand, diag_out

    items = (leaf_masked, link_parent, link_grand, leaf_inverse, col_mid, col_up, cross_mid, diag_mid, diag_up, mask_mid)
    items = tuple(jnp.moveaxis(item, 1, 0) for item in items)
    col_leaf, cross_leaf_mid, cross_leaf_top, diag_leaf = lax.map(leaf_work, items)
    col_leaf = jnp.moveaxis(col_leaf, 0, 1).reshape(2, N_LEAF * root_width, B)
    cross_leaf_mid = jnp.moveaxis(cross_leaf_mid, 0, 1).reshape(2, N_LEAF * B, B)
    cross_leaf_top = jnp.moveaxis(cross_leaf_top, 0, 1).reshape(2, N_LEAF * B, B)
    diag_leaf = jnp.moveaxis(diag_leaf, 0, 1).reshape(2, N_LEAF * B, B)
    return (col_top.reshape(2, N_TOP * root_width, B), diag_top.reshape(2, N_TOP * B, B),
            col_mid.reshape(2, N_MID * root_width, B), cross_mid.reshape(2, N_MID * B, B), diag_mid.reshape(2, N_MID * B, B),
            col_leaf, cross_leaf_mid, cross_leaf_top, diag_leaf)
```

```python
import jax
import jax.numpy as jnp
from jax import lax
from jax.experimental import pallas as pl
from jax.experimental.pallas import tpu as pltpu
from jax.sharding import PartitionSpec as P

F32 = jnp.float32
BF16 = jnp.bfloat16
BLK = 128
VMEM_LIMIT = 40 * 1024 * 1024


def swap(x, apart):
    return lax.ppermute(x, "row", [(i, i ^ apart) for i in range(lax.axis_size("row"))])


def swap_by_core(x, apart_even, apart_odd):
    return lax.ppermute(
        x,
        "row",
        [(i, i ^ (apart_odd if i & 1 else apart_even)) for i in range(lax.axis_size("row"))],
    )


def halves(x):
    hi = x.astype(BF16)
    return hi, (x - hi.astype(F32)).astype(BF16)


def mm(a, b):
    return jnp.dot(a, b, preferred_element_type=F32)


def mm3(ah, al, bh, bl):
    return mm(ah, bh) + (mm(ah, bl) + mm(al, bh))


def own_plane(device, planes):
    return (device // 4) if planes else device * 0


def pack_kernel(mine, other, z1, z2, z3):
    device = lax.axis_index("row")
    core = device % 2
    plane = device // 4
    for ref, which in ((mine, core), (other, 1 - core)):
        rows = pl.ds(pl.multiple_of(which * 32, 32), 32)

        def block(apart):
            return ref[:, :, pl.ds(pl.multiple_of((plane ^ apart) * BLK, BLK), BLK)]

        same = block(0)
        z1[:, rows, 0:128] = same
        z1[:, rows, 128:256] = block(3)
        z1[:, rows, 256:384] = block(2)
        z2[:, rows, 0:128] = same
        z2[:, rows, 128:256] = block(1)
        z3[:, rows, :] = same


def pack(mine, other):
    return pl.pallas_call(
        pack_kernel,
        out_shape=tuple(jax.ShapeDtypeStruct((2, 64, BLK * n), F32) for n in (3, 2, 1)),
        name="pack_root",
    )(mine, other)


def put_rhs(ref_h, ref_l, row, re, im):
    rh, rl = halves(re)
    ih, il = halves(im)
    for ref, r, i in ((ref_h, rh, ih), (ref_l, rl, il)):
        ref[row : row + 128, 0:128] = r
        ref[row : row + 128, 128:256] = i
        ref[row + 128 : row + 256, 0:128] = -i
        ref[row + 128 : row + 256, 128:256] = r


def put_pair(ref_h, ref_l, row, col, re, im):
    n = re.shape[0]
    rh, rl = halves(re)
    ih, il = halves(im)
    for ref, r, i in ((ref_h, rh, ih), (ref_l, rl, il)):
        ref[row : row + n, col : col + 128] = r
        ref[row : row + n, col + 128 : col + 256] = i


def put_transposed(ref_h, ref_l, row, re, im):
    for part, x in ((0, re), (1, im)):
        for r in range(4):
            xh, xl = halves(x[r * 128 : (r + 1) * 128].T)
            ref_h[row + part * 128 : row + part * 128 + 128, r * 128 : (r + 1) * 128] = xh
            ref_l[row + part * 128 : row + part * 128 + 128, r * 128 : (r + 1) * 128] = xl


def make_front_kernel(planes):
    def kernel(
        pat, pt0, pt1, pt2, pt3, it0, it1, it2, it3, pm0, pm1, lm0, lm1, im0, im1,
        panel, link_c, link_e, inv,
        xtop_h, xtop_l, ttop_h, ttop_l, xleaf_h, xleaf_l, tleaf_h, tleaf_l,
        base_top, base_leaf,
        l_s, b_s, t0_s, a_s, d_s, lhs_h, lhs_l, rhs_h, rhs_l, aux_h, aux_l,
    ):
        device = lax.axis_index("row")
        plane = own_plane(device, planes)
        quarter = device % 4
        half = device % 2
        node = device // 4

        def keep(supernode):
            return pat[node, supernode].astype(F32)

        @pl.when(pl.program_id(0) == 0)
        def _():
            for k, (p_ref, i_ref) in enumerate(((pt0, it0), (pt1, it1), (pt2, it2), (pt3, it3))):
                q = quarter ^ k
                l_s[:, pl.ds(pl.multiple_of((q ^ plane) * 128, 128), 128), :] = p_ref[...] * keep(q)
                t0_s[:, pl.ds(pl.multiple_of(q * 32, 32), 32), :] = i_ref[...]
            for k, (p_ref, a_ref, d_ref) in enumerate(((pm0, lm0, im0), (pm1, lm1, im1))):
                h = half ^ k
                for n in (0, 1):
                    s = h * 2 + n
                    b_s[:, pl.ds(pl.multiple_of((s ^ plane) * 128, 128), 128), :] = (
                        p_ref[:, n * 128 : n * 128 + 128, :] * keep(s)
                    )
                rows = pl.ds(pl.multiple_of(h * 64, 64), 64)
                a_s[:, rows, :] = a_ref[...]
                d_s[:, rows, :] = d_ref[...]
            put_pair(lhs_h, lhs_l, 0, 256, l_s[0], l_s[1])
            put_pair(lhs_h, lhs_l, 640, 256, t0_s[0], t0_s[1])
            put_rhs(rhs_h, rhs_l, 0, a_s[0], a_s[1])
            ah, al = rhs_h[0:256, :], rhs_l[0:256, :]
            got = mm3(lhs_h[0:512, 256:512], lhs_l[0:512, 256:512], ah, al)
            bt_r = b_s[0] - got[:, 0:128]
            bt_i = b_s[1] - got[:, 128:256]
            put_pair(lhs_h, lhs_l, 0, 0, bt_r, bt_i)
            put_transposed(ttop_h, ttop_l, 0, l_s[0], l_s[1])
            put_transposed(ttop_h, ttop_l, 256, bt_r, bt_i)
            for out, src in ((xtop_h, lhs_h), (xtop_l, lhs_l)):
                out[0] = src[0:512, 256:512]
                out[1] = src[0:512, 0:256]
            got = mm3(lhs_h[640:768, 256:512], lhs_l[640:768, 256:512], ah, al)
            q_r, q_i = -got[:, 0:128], -got[:, 128:256]
            put_pair(lhs_h, lhs_l, 640, 0, q_r, q_i)
            put_pair(lhs_h, lhs_l, 512, 256, q_r.T, q_i.T)
            put_rhs(rhs_h, rhs_l, 0, q_r, q_i)
            put_pair(aux_h, aux_l, 0, 0, a_s[0].T, a_s[1].T)
            got = mm3(aux_h[:, 0:256], aux_l[:, 0:256], rhs_h[0:256, :], rhs_l[0:256, :])
            d_r, d_i = d_s[0] - got[:, 0:128], d_s[1] - got[:, 128:256]
            put_pair(lhs_h, lhs_l, 512, 0, d_r, d_i)
            base_top[0] = t0_s[...]
            base_top[1, 0] = q_r
            base_top[1, 1] = q_i
            base_top[2, 0] = d_r
            base_top[2, 1] = d_i

        put_rhs(rhs_h, rhs_l, 0, link_c[0], link_c[1])
        put_rhs(rhs_h, rhs_l, 256, link_e[0], link_e[1])
        got = mm3(lhs_h[...], lhs_l[...], rhs_h[...], rhs_l[...])
        parts = []
        for part in (0, 1):
            rows = []
            for r in range(4):
                s = plane ^ r
                g = panel[part, pl.ds(pl.multiple_of(s * 128, 128), 128), :] * keep(s)
                rows.append(g - got[r * 128 : (r + 1) * 128, part * 128 : (part + 1) * 128])
            parts.append(jnp.concatenate(rows, axis=0))
        g_r, g_i = parts
        gh, gl = halves(g_r)
        xleaf_h[0, :, 0:128] = gh
        xleaf_l[0, :, 0:128] = gl
        gh, gl = halves(g_i)
        xleaf_h[0, :, 128:256] = gh
        xleaf_l[0, :, 128:256] = gl
        put_transposed(tleaf_h.at[0], tleaf_l.at[0], 0, g_r, g_i)
        r_r, r_i = -got[512:640, 0:128], -got[512:640, 128:256]
        s_r, s_i = -got[640:768, 0:128], -got[640:768, 128:256]
        put_rhs(rhs_h, rhs_l, 0, r_r, r_i)
        put_rhs(rhs_h, rhs_l, 256, s_r, s_i)
        put_pair(aux_h, aux_l, 0, 0, link_c[0].T, link_c[1].T)
        put_pair(aux_h, aux_l, 0, 256, link_e[0].T, link_e[1].T)
        got = mm3(aux_h[...], aux_l[...], rhs_h[...], rhs_l[...])
        base_leaf[0, 0, 0] = s_r
        base_leaf[0, 0, 1] = s_i
        base_leaf[0, 1, 0] = r_r
        base_leaf[0, 1, 1] = r_i
        base_leaf[0, 2, 0] = inv[0] - got[:, 0:128]
        base_leaf[0, 2, 1] = inv[1] - got[:, 128:256]

    return kernel


def whole(shape):
    return pl.BlockSpec(shape, lambda j: (0,) * len(shape))


def front(planes, pattern, tops, invs, mids, panel_leaf, link_c, link_e, inv_leaf):
    leaves = panel_leaf.shape[1] // 512
    vm = [whole(x.shape) for x in (*tops, *invs, *mids)]
    node = lambda rows: pl.BlockSpec((2, rows, BLK), lambda j: (0, j, 0))
    out = [
        ((2, 512, 256), BF16, None), ((2, 512, 256), BF16, None),
        ((512, 512), BF16, None), ((512, 512), BF16, None),
        ((leaves, 512, 256), BF16, 1), ((leaves, 512, 256), BF16, 1),
        ((leaves, 256, 512), BF16, 1), ((leaves, 256, 512), BF16, 1),
        ((3, 2, 128, 128), F32, None), ((leaves, 3, 2, 128, 128), F32, 1),
    ]
    def spec(shape, blocked):
        if blocked is None:
            return whole(shape)
        return pl.BlockSpec((1,) + shape[1:], lambda j: (j,) + (0,) * (len(shape) - 1))
    return pl.pallas_call(
        make_front_kernel(planes),
        grid=(leaves,),
        out_shape=tuple(jax.ShapeDtypeStruct(s, d) for s, d, _ in out),
        in_specs=[pl.BlockSpec(memory_space=pltpu.SMEM), *vm, node(512), node(128), node(128), node(128)],
        out_specs=tuple(spec(s, b) for s, _, b in out),
        scratch_shapes=[
            pltpu.VMEM((2, 512, 128), F32), pltpu.VMEM((2, 512, 128), F32),
            pltpu.VMEM((2, 128, 128), F32), pltpu.VMEM((2, 128, 128), F32), pltpu.VMEM((2, 128, 128), F32),
            pltpu.VMEM((768, 512), BF16), pltpu.VMEM((768, 512), BF16),
            pltpu.VMEM((512, 256), BF16), pltpu.VMEM((512, 256), BF16),
            pltpu.VMEM((128, 512), BF16), pltpu.VMEM((128, 512), BF16),
        ],
        compiler_params=pltpu.CompilerParams(vmem_limit_bytes=VMEM_LIMIT),
        cost_estimate=pl.CostEstimate(flops=2_000_000_000, bytes_accessed=9_000_000, transcendentals=0),
        name="front",
    )(pattern, *tops, *invs, *mids, panel_leaf, link_c, link_e, inv_leaf)


def make_back_kernel(planes):
    def kernel(
        pat, o0, o1, o2, o3, z1a, z1b, z2a, z2b, z3a, z3b,
        xtop_h, xtop_l, ttop_h, ttop_l, xleaf_h, xleaf_l, tleaf_h, tleaf_l, base_top, base_leaf,
        col_top, diag_top, col_mid, cross_mid, diag_mid, col_leaf, cross_c, cross_e, diag_leaf,
        own, z1, z2, z3, a_h, a_l, cb_h, cb_l, c_s, d_s,
    ):
        device = lax.axis_index("row")
        plane = own_plane(device, planes)
        quarter = device % 4
        half = device % 2
        node = device // 4

        def keep(supernode):
            return pat[node, supernode].astype(F32)

        def put(r, c, part, x):
            xh, xl = halves(x)
            rows = slice(part * 512 + r * 128, part * 512 + r * 128 + 128)
            a_h[rows, c * 128 : c * 128 + 128] = xh
            a_l[rows, c * 128 : c * 128 + 128] = xl

        def both(r, c, part, x):
            put(r, c, part, x)
            if r != c:
                put(c, r, part, x.T)

        def columns(x_h, x_l):
            got = mm3(a_h[...], a_l[...], x_h, x_l)
            re = got[0:512, 0:128] - got[512:1024, 128:256]
            im = got[0:512, 128:256] + got[512:1024, 0:128]
            res = []
            for part, x in ((0, re), (1, im)):
                rows = [x[r * 128 : r * 128 + 128] * (-keep(plane ^ r)) for r in range(4)]
                for r in range(4):
                    hi, lo = halves(rows[r])
                    cb_h[r * 128 : r * 128 + 128, part * 128 : part * 128 + 128] = hi
                    cb_l[r * 128 : r * 128 + 128, part * 128 : part * 128 + 128] = lo
                res.append(rows)
            return res

        def against(t_h, t_l):
            got = mm3(t_h, t_l, cb_h[...], cb_l[...])
            outs = []
            for n in range(t_h.shape[0] // 256):
                g = got[n * 256 : n * 256 + 256]
                outs.append((g[0:128, 0:128] - g[128:256, 128:256], g[0:128, 128:256] + g[128:256, 0:128]))
            return outs

        @pl.when(pl.program_id(0) == 0)
        def _():
            for k, ref in enumerate((o0, o1, o2, o3)):
                own[:, pl.ds(pl.multiple_of((quarter ^ k) * 32, 32), 32), :] = ref[...]
            side = (quarter // 2) ^ half
            for k, refs in enumerate(((z1a, z2a, z3a), (z1b, z2b, z3b))):
                rows = pl.ds(pl.multiple_of((side ^ k) * 64, 64), 64)
                for dst, src in zip((z1, z2, z3), refs):
                    dst[:, rows, :] = src[...]
            for part in (0, 1):
                for r in range(4):
                    both(0, r, part, own[part, :, pl.ds(pl.multiple_of((plane ^ r) * 128, 128), 128)])
                for n, c in enumerate((1, 2, 3)):
                    both(1, c, part, z1[part, :, n * 128 : n * 128 + 128])
                for n, c in enumerate((2, 3)):
                    both(2, c, part, z2[part, :, n * 128 : n * 128 + 128])
                both(3, 3, part, z3[part])
            res = columns(xtop_h[0], xtop_l[0])
            for part in (0, 1):
                for r in range(4):
                    c_s[part, pl.ds(pl.multiple_of((plane ^ r) * 128, 128), 128), :] = res[part][r]
            col_top[...] = c_s[:, pl.ds(pl.multiple_of(quarter * 128, 128), 128), :]
            (z,) = against(ttop_h[0:256], ttop_l[0:256])
            for part in (0, 1):
                d_s[part] = base_top[0, part] - z[part]
            diag_top[...] = d_s[:, pl.ds(pl.multiple_of(quarter * 32, 32), 32), :]
            res = columns(xtop_h[1], xtop_l[1])
            for part in (0, 1):
                for r in range(4):
                    c_s[part, pl.ds(pl.multiple_of((plane ^ r) * 128, 128), 128), :] = res[part][r]
            col_mid[...] = c_s[:, pl.ds(pl.multiple_of(half * 256, 256), 256), :]
            zs = against(ttop_h[...], ttop_l[...])
            rows = pl.ds(pl.multiple_of(half * 64, 64), 64)
            for n, out in ((0, cross_mid), (1, diag_mid)):
                for part in (0, 1):
                    d_s[part] = base_top[1 + n, part] - zs[n][part]
                out[...] = d_s[:, rows, :]

        res = columns(xleaf_h[0], xleaf_l[0])
        for part in (0, 1):
            for r in range(4):
                col_leaf[part, pl.ds(pl.multiple_of((plane ^ r) * 128, 128), 128), :] = res[part][r]
        z_e, z_c = against(ttop_h[...], ttop_l[...])
        (z_d,) = against(tleaf_h[0], tleaf_l[0])
        for part in (0, 1):
            cross_e[part] = base_leaf[0, 0, part] - z_e[part]
            cross_c[part] = base_leaf[0, 1, part] - z_c[part]
            diag_leaf[part] = base_leaf[0, 2, part] - z_d[part]

    return kernel


def back(planes, pattern, root, firsts):
    leaves = firsts[4].shape[0]
    vm = [whole(x.shape) for x in root]
    def blocked(x):
        return pl.BlockSpec((1,) + x.shape[1:], lambda j: (j,) + (0,) * (len(x.shape) - 1))
    xs = [whole(x.shape) for x in firsts[:4]] + [blocked(x) for x in firsts[4:8]]
    xs += [whole(firsts[8].shape), blocked(firsts[9])]
    top = [(2, 128, 128), (2, 32, 128), (2, 256, 128), (2, 64, 128), (2, 64, 128)]
    leaf = [512, 128, 128, 128]
    return pl.pallas_call(
        make_back_kernel(planes),
        grid=(leaves,),
        out_shape=tuple(jax.ShapeDtypeStruct(s, F32) for s in top)
        + tuple(jax.ShapeDtypeStruct((2, leaves * n, 128), F32) for n in leaf),
        in_specs=[pl.BlockSpec(memory_space=pltpu.SMEM), *vm, *xs],
        out_specs=tuple(whole(s) for s in top)
        + tuple(pl.BlockSpec((2, n, 128), lambda j: (0, j, 0)) for n in leaf),
        scratch_shapes=[
            pltpu.VMEM((2, 128, 512), F32), pltpu.VMEM((2, 128, 384), F32),
            pltpu.VMEM((2, 128, 256), F32), pltpu.VMEM((2, 128, 128), F32),
            pltpu.VMEM((1024, 512), BF16), pltpu.VMEM((1024, 512), BF16),
            pltpu.VMEM((512, 256), BF16), pltpu.VMEM((512, 256), BF16),
            pltpu.VMEM((2, 512, 128), F32), pltpu.VMEM((2, 128, 128), F32),
        ],
        compiler_params=pltpu.CompilerParams(vmem_limit_bytes=VMEM_LIMIT),
        cost_estimate=pl.CostEstimate(flops=8_000_000_000, bytes_accessed=12_000_000, transcendentals=0),
        name="back",
    )(pattern, *root, *firsts)


def root_by_planes(ainv_root):
    other = swap(ainv_root, 1)
    sent = pack(ainv_root, other)
    got = [swap_by_core(x, 4 * k, 4 * k + 2) for k, x in zip((1, 2, 3), sent)]
    far = swap(ainv_root, 2)
    root = [ainv_root, other, far, swap(far, 1)]
    for x in got:
        root += [x, swap(x, 1)]
    return root


def root_gathered(ainv_root):
    device = lax.axis_index("row")
    full = lax.all_gather(ainv_root, "row", axis=1, tiled=True)
    quarter = device % 4
    side = (quarter // 2) ^ (device % 2)
    root = [lax.dynamic_slice_in_dim(full, (quarter ^ k) * 32, 32, 1) for k in range(4)]
    for r in (1, 2, 3):
        for k in (0, 1):
            root.append(
                lax.dynamic_slice_in_dim(full[:, :, r * 128 :], r * 128 + (side ^ k) * 64, 64, 1)
            )
    return root


def local(
    ainv_root, pattern, panel_top, inv_top, panel_mid, link_mid, inv_mid,
    panel_leaf, link_leaf_mid, link_leaf_top, inv_leaf,
):
    planes = lax.axis_size("row") == 16
    root = root_by_planes(ainv_root) if planes else root_gathered(ainv_root)
    tops, invs, mids = [], [], []
    for x, pieces in ((panel_top, tops), (inv_top, invs)):
        far = swap(x, 2)
        pieces += [x, swap(x, 1), far, swap(far, 1)]
    for x in (panel_mid, link_mid, inv_mid):
        mids += [x, swap(x, 1)]
    firsts = front(planes, pattern, tops, invs, mids, panel_leaf, link_leaf_mid, link_leaf_top, inv_leaf)
    return back(planes, pattern, root, firsts)


def solution(mesh):
    split = P("pole", "row", None)
    return jax.shard_map(
        local,
        mesh=mesh,
        in_specs=(split, P()) + (split,) * 9,
        out_specs=(split,) * 9,
        check_vma=False,
    )
```

```python
import jax
import jax.numpy as jnp
from jax import lax
from jax.experimental import pallas as pl
from jax.experimental.pallas import tpu as pltpu
from jax.sharding import PartitionSpec as P

F32 = jnp.float32
BF16 = jnp.bfloat16
ANY = pl.BlockSpec(memory_space=pl.ANY)
VMEM = pl.BlockSpec(memory_space=pltpu.VMEM)


def swap(x, apart):
    return lax.ppermute(x, "row", [(i, i ^ apart) for i in range(lax.axis_size("row"))])


def swap_by_core(x, apart_even, apart_odd):
    return lax.ppermute(
        x,
        "row",
        [(i, i ^ (apart_odd if i & 1 else apart_even)) for i in range(lax.axis_size("row"))],
    )


def halves(x):
    hi = x.astype(BF16)
    return hi, (x - hi.astype(F32)).astype(BF16)


def mm(a, b):
    return jnp.dot(a, b, preferred_element_type=F32)


def mm3(ah, al, bh, bl):
    return mm(ah, bh) + (mm(ah, bl) + mm(al, bh))


def at(start, size):
    return pl.ds(pl.multiple_of(start, size), size)


def in_hbm(x):
    return pltpu.with_memory_space_constraint(x, pltpu.HBM)


def own_plane(device, planes):
    return device // 4 if planes else device * 0


def pack_kernel(
    pat, a_hbm, a_other, t_hbm, i_hbm, pm_hbm, lm_hbm, im_hbm,
    z1, z2, z3, mine_top, mine_mid, masks, a, pat_s, sem,
):
    device = lax.axis_index("row")
    core = device % 2
    plane = device // 4
    pairs = (
        (a_hbm, a), (pat, pat_s),
        (t_hbm, mine_top.at[:, 0:128, :]), (i_hbm, mine_top.at[:, 128:160, :]),
        (pm_hbm, mine_mid.at[:, 0:256, :]), (lm_hbm, mine_mid.at[:, 256:320, :]),
        (im_hbm, mine_mid.at[:, 320:384, :]),
    )
    copies = [pltpu.make_async_copy(src, dst, sem.at[n]) for n, (src, dst) in enumerate(pairs)]
    for copy in copies:
        copy.start()
    for n, (ref, which) in enumerate(((a_other, 1 - core), (a, core))):
        if n == 1:
            copies[0].wait()
        rows = at(which * 32, 32)

        def block(apart):
            return ref[:, :, at((plane ^ apart) * 128, 128)]

        same = block(0)
        z1[:, rows, 0:128] = same
        z1[:, rows, 128:256] = block(3)
        z1[:, rows, 256:384] = block(2)
        z2[:, rows, 0:128] = same
        z2[:, rows, 128:256] = block(1)
        z3[:, rows, :] = same
    copies[1].wait()
    for r in range(4):
        masks[r : r + 1, :] = jnp.full((1, 128), pat_s[plane, plane ^ r], jnp.int32).astype(F32)
    masks[4:8, :] = jnp.zeros((4, 128), F32)
    for copy in copies[2:]:
        copy.wait()


def pack(pattern, a, a_other, *mine):
    shapes = [(2, 64, 384), (2, 64, 256), (2, 64, 128), (2, 160, 128), (2, 384, 128), (8, 128)]
    return pl.pallas_call(
        pack_kernel,
        out_shape=tuple(jax.ShapeDtypeStruct(s, F32) for s in shapes),
        in_specs=[ANY, ANY, VMEM] + [ANY] * 5,
        out_specs=(VMEM,) * len(shapes),
        scratch_shapes=[pltpu.VMEM(a.shape, F32), pltpu.SMEM(pattern.shape, jnp.int32), pltpu.SemaphoreType.DMA((7,))],
        compiler_params=pltpu.CompilerParams(vmem_limit_bytes=4 << 20),
        name="pack_sent",
    )(in_hbm(pattern), in_hbm(a), a_other, *(in_hbm(x) for x in mine))


def put_rhs(ref_h, ref_l, row, re, im):
    rh, rl = halves(re)
    ih, il = halves(im)
    for ref, r, i in ((ref_h, rh, ih), (ref_l, rl, il)):
        ref[row : row + 128, 0:128] = r
        ref[row : row + 128, 128:256] = i
        ref[row + 128 : row + 256, 0:128] = -i
        ref[row + 128 : row + 256, 128:256] = r


def put_pair(ref_h, ref_l, row, col, re, im):
    n = re.shape[0]
    rh, rl = halves(re)
    ih, il = halves(im)
    for ref, r, i in ((ref_h, rh, ih), (ref_l, rl, il)):
        ref[row : row + n, col : col + 128] = r
        ref[row : row + n, col + 128 : col + 256] = i


def put_transposed(ref_h, ref_l, row, r, re, im):
    for part, x in ((0, re), (128, im)):
        xh, xl = halves(x.T)
        ref_h[row + part : row + part + 128, r * 128 : r * 128 + 128] = xh
        ref_l[row + part : row + part + 128, r * 128 : r * 128 + 128] = xl


def make_front_kernel(planes, leaves):
    def kernel(
        mask_ref, top0, top1, top2, top3, mid0, mid1, panel, link_c, link_e, inv,
        x_h, x_l, tt_h, tt_l, tl_h, tl_l, base_top, base_leaf,
        l_s, b_s, t0_s, am_s, d_s, g_s, lc_s, le_s, li_s,
        lhs_h, lhs_l, ra_h, ra_l, rq_h, rq_l, aux_h, aux_l, rhs_h, rhs_l, rrs_h, rrs_l, auxl_h, auxl_l, sem,
    ):
        device = lax.axis_index("row")
        plane = own_plane(device, planes)
        quarter = device % 4
        half = device % 2
        copies = []

        def fetch(src, dst):
            copy = pltpu.make_async_copy(src, dst, sem.at[len(copies)])
            copy.start()
            copies.append(copy)
            return copy

        def rel(supernode):
            return at((supernode ^ plane) * 128, 128)

        links = [fetch(link_c, lc_s), fetch(link_e, le_s)]
        panels = [fetch(panel.at[:, j * 512 : j * 512 + 512, :], g_s.at[:, j * 512 : j * 512 + 512, :]) for j in range(leaves)]
        fetch(inv, li_s)
        for k, ref in enumerate((top0, top1, top2, top3)):
            l_s[:, rel(quarter ^ k), :] = ref[:, 0:128, :]
            t0_s[:, at((quarter ^ k) * 32, 32), :] = ref[:, 128:160, :]
        for k, ref in enumerate((mid0, mid1)):
            h = half ^ k
            for n in (0, 1):
                b_s[:, rel(h * 2 + n), :] = ref[:, n * 128 : n * 128 + 128, :]
            am_s[:, at(h * 64, 64), :] = ref[:, 256:320, :]
            d_s[:, at(h * 64, 64), :] = ref[:, 320:384, :]
        masks = [mask_ref[r : r + 1, :] for r in range(4)]

        def put_x(j, r, re, im):
            put_rhs(x_h.at[j], x_l.at[j], r * 256, re, im)

        put_rhs(ra_h, ra_l, 0, am_s[0], am_s[1])
        for r in range(4):
            rows = slice(r * 128, r * 128 + 128)
            re, im = l_s[0, rows] * masks[r], l_s[1, rows] * masks[r]
            put_pair(lhs_h, lhs_l, r * 128, 256, re, im)
            put_x(0, r, re, im)
            put_transposed(tt_h, tt_l, 0, r, re, im)
        put_pair(lhs_h, lhs_l, 640, 256, t0_s[0], t0_s[1])
        ah, al = ra_h[...], ra_l[...]
        got = mm3(lhs_h[0:512, 256:512], lhs_l[0:512, 256:512], ah, al)
        for r in range(4):
            rows = slice(r * 128, r * 128 + 128)
            re = b_s[0, rows] * masks[r] - got[rows, 0:128]
            im = b_s[1, rows] * masks[r] - got[rows, 128:256]
            put_pair(lhs_h, lhs_l, r * 128, 0, re, im)
            put_x(1, r, re, im)
            put_transposed(tt_h, tt_l, 256, r, re, im)
        got = mm3(lhs_h[640:768, 256:512], lhs_l[640:768, 256:512], ah, al)
        q_r, q_i = -got[:, 0:128], -got[:, 128:256]
        put_pair(lhs_h, lhs_l, 640, 0, q_r, q_i)
        put_pair(lhs_h, lhs_l, 512, 256, q_r.T, q_i.T)
        put_rhs(rq_h, rq_l, 0, q_r, q_i)
        put_pair(aux_h, aux_l, 0, 0, am_s[0].T, am_s[1].T)
        got = mm3(aux_h[...], aux_l[...], rq_h[...], rq_l[...])
        d_r, d_i = d_s[0] - got[:, 0:128], d_s[1] - got[:, 128:256]
        put_pair(lhs_h, lhs_l, 512, 0, d_r, d_i)
        base_top[0] = t0_s[...]
        base_top[1, 0] = q_r
        base_top[1, 1] = q_i
        base_top[2, 0] = d_r
        base_top[2, 1] = d_i

        for copy in links:
            copy.wait()
        for j in range(leaves):
            mine = slice(j * 128, j * 128 + 128)
            put_rhs(rhs_h.at[j], rhs_l.at[j], 0, lc_s[0, mine], lc_s[1, mine])
            put_rhs(rhs_h.at[j], rhs_l.at[j], 256, le_s[0, mine], le_s[1, mine])
            put_pair(auxl_h.at[j], auxl_l.at[j], 0, 0, lc_s[0, mine].T, lc_s[1, mine].T)
            put_pair(auxl_h.at[j], auxl_l.at[j], 0, 256, le_s[0, mine].T, le_s[1, mine].T)
        for j in range(leaves):
            panels[j].wait()
            got = mm3(lhs_h[...], lhs_l[...], rhs_h[j], rhs_l[j])
            for r in range(4):
                rows = slice(r * 128, r * 128 + 128)
                mine = at(j * 512 + (plane ^ r) * 128, 128)
                re = g_s[0, mine] * masks[r] - got[rows, 0:128]
                im = g_s[1, mine] * masks[r] - got[rows, 128:256]
                put_x(2 + j, r, re, im)
                put_transposed(tl_h.at[j], tl_l.at[j], 0, r, re, im)
            r_r, r_i = -got[512:640, 0:128], -got[512:640, 128:256]
            s_r, s_i = -got[640:768, 0:128], -got[640:768, 128:256]
            put_rhs(rrs_h.at[j], rrs_l.at[j], 0, r_r, r_i)
            put_rhs(rrs_h.at[j], rrs_l.at[j], 256, s_r, s_i)
            base_leaf[j, 0, 0] = s_r
            base_leaf[j, 0, 1] = s_i
            base_leaf[j, 1, 0] = r_r
            base_leaf[j, 1, 1] = r_i
        copies[-1].wait()
        for j in range(leaves):
            mine = slice(j * 128, j * 128 + 128)
            got = mm3(auxl_h[j], auxl_l[j], rrs_h[j], rrs_l[j])
            base_leaf[j, 2, 0] = li_s[0, mine] - got[:, 0:128]
            base_leaf[j, 2, 1] = li_s[1, mine] - got[:, 128:256]

    return kernel


def front(planes, masks, tops, mids, panel_leaf, link_c, link_e, inv_leaf):
    leaves = panel_leaf.shape[1] // 512
    n = leaves + 2
    v = pltpu.VMEM
    out = [
        ((n, 1024, 256), BF16), ((n, 1024, 256), BF16), ((512, 512), BF16), ((512, 512), BF16),
        ((leaves, 256, 512), BF16), ((leaves, 256, 512), BF16),
        ((3, 2, 128, 128), F32), ((leaves, 3, 2, 128, 128), F32),
    ]
    pair = lambda *shape: [v(shape, BF16)] * 2
    return pl.pallas_call(
        make_front_kernel(planes, leaves),
        out_shape=tuple(jax.ShapeDtypeStruct(s, d) for s, d in out),
        in_specs=[VMEM] * 7 + [ANY] * 4,
        out_specs=(VMEM,) * len(out),
        scratch_shapes=[
            v((2, 512, 128), F32), v((2, 512, 128), F32),
            v((2, 128, 128), F32), v((2, 128, 128), F32), v((2, 128, 128), F32),
            v((2, leaves * 512, 128), F32),
            v((2, leaves * 128, 128), F32), v((2, leaves * 128, 128), F32), v((2, leaves * 128, 128), F32),
            *pair(768, 512), *pair(256, 256), *pair(256, 256), *pair(128, 256),
            *pair(leaves, 512, 256), *pair(leaves, 512, 256), *pair(leaves, 128, 512),
            pltpu.SemaphoreType.DMA((3 + leaves,)),
        ],
        compiler_params=pltpu.CompilerParams(vmem_limit_bytes=24 << 20),
        cost_estimate=pl.CostEstimate(flops=1_000_000, bytes_accessed=1_000, transcendentals=0),
        name="front",
    )(masks, *tops, *mids, in_hbm(panel_leaf), in_hbm(link_c), in_hbm(link_e), in_hbm(inv_leaf))


def make_back_kernel(planes, leaves):
    def kernel(
        mask_ref, a0, a1, a2, a3, z1a, z1b, z2a, z2b, z3a, z3b,
        x_h, x_l, tt_h, tt_l, tl_h, tl_l, base_top, base_leaf,
        col_top, diag_top, col_mid, cross_mid, diag_mid, col_leaf, cross_c, cross_e, diag_leaf,
        own, a_h, a_l, cb_h, cb_l, c_s, d_s, e_s, f_s, top_s, mid_s, sem,
    ):
        device = lax.axis_index("row")
        plane = own_plane(device, planes)
        quarter = device % 4
        half = device % 2
        lower = (quarter // 2) ^ half == 0
        copies = []

        def move(src, dst):
            copy = pltpu.make_async_copy(src, dst, sem.at[len(copies)])
            copy.start()
            copies.append(copy)
            return copy

        raw = move(a0, own.at[:, at(quarter * 32, 32), :])
        masks = [-mask_ref[r : r + 1, :] for r in range(4)]
        for row, a_ref, b_ref, cols in ((1, z1a, z1b, (1, 2, 3)), (2, z2a, z2b, (2, 3)), (3, z3a, z3b, (3,))):
            for n, col in enumerate(cols):
                parts = []
                for part in (0, 1):
                    x = a_ref[part, :, n * 128 : n * 128 + 128]
                    y = b_ref[part, :, n * 128 : n * 128 + 128]
                    parts.append(jnp.concatenate([jnp.where(lower, x, y), jnp.where(lower, y, x)], axis=0))
                re, im = parts
                put_pair(a_h, a_l, row * 128, col * 256, re, im)
                if row != col:
                    put_pair(a_h, a_l, col * 128, row * 256, re.T, im.T)
        for k, ref in enumerate((a1, a2, a3)):
            own[:, at((quarter ^ (k + 1)) * 32, 32), :] = ref[...]
        raw.wait()
        for r in range(4):
            cols = at((plane ^ r) * 128, 128)
            re, im = own[0, :, cols], own[1, :, cols]
            put_pair(a_h, a_l, 0, r * 256, re, im)
            if r:
                put_pair(a_h, a_l, r * 128, 0, re.T, im.T)

        def columns(j, out):
            got = mm3(a_h[...], a_l[...], x_h[j], x_l[j])
            for r in range(4):
                rows = slice(r * 128, r * 128 + 128)
                place = at((plane ^ r) * 128, 128)
                for part in (0, 1):
                    lanes = slice(part * 128, part * 128 + 128)
                    c = got[rows, lanes] * masks[r]
                    hi, lo = halves(c)
                    cb_h[j, rows, lanes] = hi
                    cb_l[j, rows, lanes] = lo
                    out[part, place, :] = c

        def against(j, t_h, t_l):
            got = mm3(t_h, t_l, cb_h[j], cb_l[j])
            outs = []
            for n in range(t_h.shape[0] // 256):
                g = got[n * 256 : n * 256 + 256]
                outs.append((g[0:128, 0:128] - g[128:256, 128:256], g[0:128, 128:256] + g[128:256, 0:128]))
            return outs

        def leaf_tail(j):
            th = jnp.concatenate([tt_h[...], tl_h[j]], axis=0)
            tl = jnp.concatenate([tt_l[...], tl_l[j]], axis=0)
            zs = against(2 + j, th, tl)
            for n, (z, out) in enumerate(zip(zs, (e_s, d_s, f_s))):
                for part in (0, 1):
                    out[j, part] = base_leaf[j, n, part] - z[part]
            mine = slice(j * 128, j * 128 + 128)
            move(e_s.at[j], cross_e.at[:, mine, :])
            move(d_s.at[j], cross_c.at[:, mine, :])
            move(f_s.at[j], diag_leaf.at[:, mine, :])

        for j in range(leaves):
            columns(2 + j, c_s.at[2 + j])
            move(c_s.at[2 + j], col_leaf.at[:, j * 512 : j * 512 + 512, :])
        columns(1, c_s.at[1])
        move(c_s.at[1, :, at(half * 256, 256), :], col_mid)
        columns(0, c_s.at[0])
        move(c_s.at[0, :, at(quarter * 128, 128), :], col_top)
        for j in range(leaves):
            leaf_tail(j)
        zs = against(1, tt_h[...], tt_l[...])
        for n in (0, 1):
            for part in (0, 1):
                mid_s[n, part] = base_top[1 + n, part] - zs[n][part]
        move(mid_s.at[0, :, at(half * 64, 64), :], cross_mid)
        move(mid_s.at[1, :, at(half * 64, 64), :], diag_mid)
        (z,) = against(0, tt_h[0:256], tt_l[0:256])
        for part in (0, 1):
            top_s[part] = base_top[0, part] - z[part]
        move(top_s.at[:, at(quarter * 32, 32), :], diag_top)
        for copy in copies[1:]:
            copy.wait()

    return kernel


def back(planes, masks, own, root, firsts, leaves):
    n = leaves + 2
    v = pltpu.VMEM
    shapes = [(2, 128, 128), (2, 32, 128), (2, 256, 128), (2, 64, 128), (2, 64, 128)]
    shapes += [(2, leaves * rows, 128) for rows in (512, 128, 128, 128)]
    pair = lambda *shape: [v(shape, BF16)] * 2
    return pl.pallas_call(
        make_back_kernel(planes, leaves),
        out_shape=tuple(jax.ShapeDtypeStruct(s, F32) for s in shapes),
        in_specs=[VMEM, ANY] + [VMEM] * (9 + len(firsts)),
        out_specs=(ANY,) * len(shapes),
        scratch_shapes=[
            v((2, 128, 512), F32), *pair(512, 1024), *pair(n, 512, 256), v((n, 2, 512, 128), F32),
            v((leaves, 2, 128, 128), F32), v((leaves, 2, 128, 128), F32), v((leaves, 2, 128, 128), F32),
            v((2, 128, 128), F32), v((2, 2, 128, 128), F32),
            pltpu.SemaphoreType.DMA((10 + 4 * leaves,)),
        ],
        compiler_params=pltpu.CompilerParams(vmem_limit_bytes=24 << 20),
        cost_estimate=pl.CostEstimate(flops=8_000_000_000, bytes_accessed=12_000_000, transcendentals=0),
        name="back",
    )(masks, in_hbm(own[0]), *own[1:], *root, *firsts)


def root_gathered(ainv_root):
    device = lax.axis_index("row")
    full = lax.all_gather(ainv_root, "row", axis=1, tiled=True)
    quarter = device % 4
    side = (quarter // 2) ^ (device % 2)
    own = [lax.dynamic_slice_in_dim(full, (quarter ^ k) * 32, 32, 1) for k in range(4)]
    root = []
    for r in (1, 2, 3):
        for k in (0, 1):
            root.append(
                lax.dynamic_slice_in_dim(full[:, :, r * 128 :], r * 128 + (side ^ k) * 64, 64, 1)
            )
    return own, root


def local(
    ainv_root, pattern, panel_top, inv_top, panel_mid, link_mid, inv_mid,
    panel_leaf, link_leaf_mid, link_leaf_top, inv_leaf,
):
    planes = lax.axis_size("row") == 16
    leaves = panel_leaf.shape[1] // 512
    if planes:
        a_other = swap(ainv_root, 1)
        *sent, top, mid, masks = pack(
            pattern, ainv_root, a_other, panel_top, inv_top, panel_mid, link_mid, inv_mid
        )
        got = [swap_by_core(x, 4 * k, 4 * k + 2) for k, x in zip((1, 2, 3), sent)]
        a_far = swap(ainv_root, 2)
        own = [ainv_root, a_other, a_far, swap(a_far, 1)]
    else:
        top = jnp.concatenate([panel_top, inv_top], axis=1)
        mid = jnp.concatenate([panel_mid, link_mid, inv_mid], axis=1)
        node = lax.dynamic_index_in_dim(pattern, lax.axis_index("row") // 4, 0, keepdims=False)
        masks = jnp.broadcast_to(jnp.pad(node.astype(F32), (0, 4))[:, None], (8, 128))
        own, root = root_gathered(ainv_root)
    far = swap(top, 2)
    firsts = front(
        planes, masks, [top, swap(top, 1), far, swap(far, 1)], [mid, swap(mid, 1)],
        panel_leaf, link_leaf_mid, link_leaf_top, inv_leaf,
    )
    if planes:
        got = lax.optimization_barrier(tuple(got) + tuple(firsts))
        firsts = got[3:]
        root = []
        for x in got[:3]:
            root += [x, swap(x, 1)]
    return back(planes, masks, own, root, firsts, leaves)


def solution(mesh):
    split = P("pole", "row", None)
    return jax.shard_map(
        local,
        mesh=mesh,
        in_specs=(split, P()) + (split,) * 9,
        out_specs=(split,) * 9,
        check_vma=False,
    )
```

```python
import jax
import jax.numpy as jnp
from jax import lax
from jax.experimental import pallas as pl
from jax.experimental.pallas import tpu as pltpu
from jax.sharding import PartitionSpec as P

F32 = jnp.float32
BF16 = jnp.bfloat16
ANY = pl.BlockSpec(memory_space=pl.ANY)
VMEM = pl.BlockSpec(memory_space=pltpu.VMEM)


def swap(x, apart):
    return lax.ppermute(x, "row", [(i, i ^ apart) for i in range(lax.axis_size("row"))])


def halves(x):
    hi = x.astype(BF16)
    return hi, (x - hi.astype(F32)).astype(BF16)


def mm(a, b):
    return jnp.dot(a, b, preferred_element_type=F32)


def mm3(ah, al, bh, bl):
    return mm(ah, bh) + (mm(ah, bl) + mm(al, bh))


def at(start, size):
    return pl.ds(pl.multiple_of(start, size), size)


def in_hbm(x):
    return pltpu.with_memory_space_constraint(x, pltpu.HBM)


def own_plane(device, planes):
    return device // 4 if planes else device * 0


def pack_kernel(pat, a_hbm, t_hbm, i_hbm, pm_hbm, lm_hbm, im_hbm, top, mid, masks, z1, z2, z3, pat_s, sem):
    plane = lax.axis_index("row") // 4
    pairs = [
        (pat, pat_s),
        (t_hbm, top.at[:, 0:128, :]), (i_hbm, top.at[:, 128:160, :]),
        (pm_hbm, mid.at[:, 0:256, :]), (lm_hbm, mid.at[:, 256:320, :]), (im_hbm, mid.at[:, 320:384, :]),
    ]
    for n in range(4):
        pairs.append((a_hbm.at[:, :, n * 128 : n * 128 + 128], top.at[:, 160 + n * 32 : 192 + n * 32, :]))
    for dst, order in ((z1, (0, 3, 2)), (z2, (0, 1)), (z3, (0,))):
        for n, apart in enumerate(order):
            pairs.append((a_hbm.at[:, :, at((plane ^ apart) * 128, 128)], dst.at[:, n * 32 : n * 32 + 32, :]))
    copies = [pltpu.make_async_copy(src, dst, sem.at[n]) for n, (src, dst) in enumerate(pairs)]
    for copy in copies:
        copy.start()
    copies[0].wait()
    for r in range(4):
        masks[r : r + 1, :] = jnp.full((1, 128), pat_s[plane, plane ^ r], jnp.int32).astype(F32)
    masks[4:8, :] = jnp.zeros((4, 128), F32)
    for copy in copies[1:]:
        copy.wait()


def pack(pattern, *mine):
    shapes = [(2, 288, 128), (2, 384, 128), (8, 128), (2, 96, 128), (2, 64, 128), (2, 32, 128)]
    return pl.pallas_call(
        pack_kernel,
        out_shape=tuple(jax.ShapeDtypeStruct(s, F32) for s in shapes),
        in_specs=[ANY] * 7,
        out_specs=(VMEM,) * len(shapes),
        scratch_shapes=[pltpu.SMEM(pattern.shape, jnp.int32), pltpu.SemaphoreType.DMA((16,))],
        compiler_params=pltpu.CompilerParams(vmem_limit_bytes=4 << 20),
        cost_estimate=pl.CostEstimate(flops=1_000_000, bytes_accessed=1_000, transcendentals=0),
        name="pack_panels",
    )(in_hbm(pattern), *(in_hbm(x) for x in mine))


def join_kernel(z1, z2, z3, joined):
    joined[:, 0:96, :] = z1[...]
    joined[:, 96:160, :] = z2[...]
    joined[:, 160:192, :] = z3[...]


def join(*blocks):
    return pl.pallas_call(
        join_kernel,
        out_shape=jax.ShapeDtypeStruct((2, 192, 128), F32),
        in_specs=[VMEM] * 3,
        out_specs=VMEM,
        compiler_params=pltpu.CompilerParams(vmem_limit_bytes=4 << 20),
        cost_estimate=pl.CostEstimate(flops=1_000_000, bytes_accessed=1_000, transcendentals=0),
        name="join_root",
    )(*blocks)


def put_rhs(ref_h, ref_l, row, re, im):
    rh, rl = halves(re)
    ih, il = halves(im)
    for ref, r, i in ((ref_h, rh, ih), (ref_l, rl, il)):
        ref[row : row + 128, 0:128] = r
        ref[row : row + 128, 128:256] = i
        ref[row + 128 : row + 256, 0:128] = -i
        ref[row + 128 : row + 256, 128:256] = r


def put_pair(ref_h, ref_l, row, col, re, im):
    n = re.shape[0]
    rh, rl = halves(re)
    ih, il = halves(im)
    for ref, r, i in ((ref_h, rh, ih), (ref_l, rl, il)):
        ref[row : row + n, col : col + 128] = r
        ref[row : row + n, col + 128 : col + 256] = i


def put_transposed(ref_h, ref_l, row, r, re, im):
    for part, x in ((0, re), (128, im)):
        xh, xl = halves(x.T)
        ref_h[row + part : row + part + 128, r * 128 : r * 128 + 128] = xh
        ref_l[row + part : row + part + 128, r * 128 : r * 128 + 128] = xl


def make_prep_kernel(leaves):
    def kernel(panel, link_c, link_e, inv, g, li, rhs_h, rhs_l, auxl_h, auxl_l, lc_s, le_s, sem):
        pairs = ((link_c, lc_s), (link_e, le_s), (panel, g), (inv, li))
        copies = [pltpu.make_async_copy(src, dst, sem.at[n]) for n, (src, dst) in enumerate(pairs)]
        for copy in copies:
            copy.start()
        for row, ref, copy in ((0, lc_s, copies[0]), (256, le_s, copies[1])):
            copy.wait()
            for j in range(leaves):
                mine = slice(j * 128, j * 128 + 128)
                re, im = ref[0, mine], ref[1, mine]
                put_rhs(rhs_h.at[j], rhs_l.at[j], row, re, im)
                put_pair(auxl_h.at[j], auxl_l.at[j], 0, row, re.T, im.T)
        copies[2].wait()
        copies[3].wait()

    return kernel


def prep(panel, link_c, link_e, inv):
    leaves = panel.shape[1] // 512
    v = pltpu.VMEM
    out = [(panel.shape, F32), (inv.shape, F32)]
    out += [((leaves, 512, 256), BF16)] * 2 + [((leaves, 128, 512), BF16)] * 2
    return pl.pallas_call(
        make_prep_kernel(leaves),
        out_shape=tuple(jax.ShapeDtypeStruct(s, d) for s, d in out),
        in_specs=[ANY] * 4,
        out_specs=(VMEM,) * len(out),
        scratch_shapes=[v(link_c.shape, F32), v(link_e.shape, F32), pltpu.SemaphoreType.DMA((4,))],
        compiler_params=pltpu.CompilerParams(vmem_limit_bytes=12 << 20),
        cost_estimate=pl.CostEstimate(flops=1_000_000, bytes_accessed=1_000, transcendentals=0),
        name="prep",
    )(in_hbm(panel), in_hbm(link_c), in_hbm(link_e), in_hbm(inv))


def make_front_kernel(planes, leaves):
    def kernel(
        mask_ref, top0, top1, top2, top3, mid0, mid1, g_s, li_s, rhs_h, rhs_l, auxl_h, auxl_l,
        x_h, x_l, tt_h, tt_l, tl_h, tl_l, base_top, base_leaf, c_own,
        l_s, b_s, t0_s, am_s, d_s, own, row_h, row_l, col_h, col_l,
        lhs_h, lhs_l, ra_h, ra_l, rq_h, rq_l, aux_h, aux_l, rrs_h, rrs_l,
    ):
        device = lax.axis_index("row")
        plane = own_plane(device, planes)
        quarter = device % 4
        half = device % 2
        def rel(supernode):
            return at((supernode ^ plane) * 128, 128)

        for k, ref in enumerate((top0, top1, top2, top3)):
            q = quarter ^ k
            l_s[:, rel(q), :] = ref[:, 0:128, :]
            t0_s[:, at(q * 32, 32), :] = ref[:, 128:160, :]
            for n in range(4):
                own[:, at(q * 32, 32), n * 128 : n * 128 + 128] = ref[:, 160 + n * 32 : 192 + n * 32, :]
        for k, ref in enumerate((mid0, mid1)):
            h = half ^ k
            for n in (0, 1):
                b_s[:, rel(h * 2 + n), :] = ref[:, n * 128 : n * 128 + 128, :]
            am_s[:, at(h * 64, 64), :] = ref[:, 256:320, :]
            d_s[:, at(h * 64, 64), :] = ref[:, 320:384, :]
        masks = [mask_ref[r : r + 1, :] for r in range(4)]

        def put_x(j, r, re, im):
            put_rhs(x_h.at[j], x_l.at[j], r * 256, re, im)

        for r in range(4):
            cols = at((plane ^ r) * 128, 128)
            re, im = own[0, :, cols], own[1, :, cols]
            put_pair(row_h, row_l, 0, r * 256, re, im)
            if r:
                put_pair(col_h, col_l, (r - 1) * 128, 0, re.T, im.T)

        def own_product(j):
            c_own[j, 0:128] = mm3(row_h[...], row_l[...], x_h[j], x_l[j])
            c_own[j, 128:512] = mm3(col_h[...], col_l[...], x_h[j, 0:256], x_l[j, 0:256])

        put_rhs(ra_h, ra_l, 0, am_s[0], am_s[1])
        for r in range(4):
            rows = slice(r * 128, r * 128 + 128)
            re, im = l_s[0, rows] * masks[r], l_s[1, rows] * masks[r]
            put_pair(lhs_h, lhs_l, r * 128, 256, re, im)
            put_x(0, r, re, im)
            put_transposed(tt_h, tt_l, 0, r, re, im)
        put_pair(lhs_h, lhs_l, 640, 256, t0_s[0], t0_s[1])
        ah, al = ra_h[...], ra_l[...]
        got = mm3(lhs_h[0:512, 256:512], lhs_l[0:512, 256:512], ah, al)
        for r in range(4):
            rows = slice(r * 128, r * 128 + 128)
            re = b_s[0, rows] * masks[r] - got[rows, 0:128]
            im = b_s[1, rows] * masks[r] - got[rows, 128:256]
            put_pair(lhs_h, lhs_l, r * 128, 0, re, im)
            put_x(1, r, re, im)
            put_transposed(tt_h, tt_l, 256, r, re, im)
        got = mm3(lhs_h[640:768, 256:512], lhs_l[640:768, 256:512], ah, al)
        q_r, q_i = -got[:, 0:128], -got[:, 128:256]
        put_pair(lhs_h, lhs_l, 640, 0, q_r, q_i)
        put_pair(lhs_h, lhs_l, 512, 256, q_r.T, q_i.T)
        put_rhs(rq_h, rq_l, 0, q_r, q_i)
        put_pair(aux_h, aux_l, 0, 0, am_s[0].T, am_s[1].T)
        got = mm3(aux_h[...], aux_l[...], rq_h[...], rq_l[...])
        d_r, d_i = d_s[0] - got[:, 0:128], d_s[1] - got[:, 128:256]
        put_pair(lhs_h, lhs_l, 512, 0, d_r, d_i)
        base_top[0] = t0_s[...]
        base_top[1, 0] = q_r
        base_top[1, 1] = q_i
        base_top[2, 0] = d_r
        base_top[2, 1] = d_i

        own_product(0)
        own_product(1)
        for j in range(leaves):
            got = mm3(lhs_h[...], lhs_l[...], rhs_h[j], rhs_l[j])
            for r in range(4):
                rows = slice(r * 128, r * 128 + 128)
                mine = at(j * 512 + (plane ^ r) * 128, 128)
                re = g_s[0, mine] * masks[r] - got[rows, 0:128]
                im = g_s[1, mine] * masks[r] - got[rows, 128:256]
                put_x(2 + j, r, re, im)
                put_transposed(tl_h.at[j], tl_l.at[j], 0, r, re, im)
            r_r, r_i = -got[512:640, 0:128], -got[512:640, 128:256]
            s_r, s_i = -got[640:768, 0:128], -got[640:768, 128:256]
            put_rhs(rrs_h.at[j], rrs_l.at[j], 0, r_r, r_i)
            put_rhs(rrs_h.at[j], rrs_l.at[j], 256, s_r, s_i)
            base_leaf[j, 0, 0] = s_r
            base_leaf[j, 0, 1] = s_i
            base_leaf[j, 1, 0] = r_r
            base_leaf[j, 1, 1] = r_i
        for j in range(leaves):
            mine = slice(j * 128, j * 128 + 128)
            got = mm3(auxl_h[j], auxl_l[j], rrs_h[j], rrs_l[j])
            base_leaf[j, 2, 0] = li_s[0, mine] - got[:, 0:128]
            base_leaf[j, 2, 1] = li_s[1, mine] - got[:, 128:256]
            own_product(2 + j)

    return kernel


def front(planes, masks, tops, mids, prepared):
    leaves = prepared[0].shape[1] // 512
    n = leaves + 2
    v = pltpu.VMEM
    out = [
        ((n, 1024, 256), BF16), ((n, 1024, 256), BF16), ((512, 512), BF16), ((512, 512), BF16),
        ((leaves, 256, 512), BF16), ((leaves, 256, 512), BF16),
        ((3, 2, 128, 128), F32), ((leaves, 3, 2, 128, 128), F32), ((n, 512, 256), F32),
    ]
    pair = lambda *shape: [v(shape, BF16)] * 2
    return pl.pallas_call(
        make_front_kernel(planes, leaves),
        out_shape=tuple(jax.ShapeDtypeStruct(s, d) for s, d in out),
        in_specs=[VMEM] * 13,
        out_specs=(VMEM,) * len(out),
        scratch_shapes=[
            v((2, 512, 128), F32), v((2, 512, 128), F32),
            v((2, 128, 128), F32), v((2, 128, 128), F32), v((2, 128, 128), F32),
            v((2, 128, 512), F32), *pair(128, 1024), *pair(384, 256),
            *pair(768, 512), *pair(256, 256), *pair(256, 256), *pair(128, 256),
            *pair(leaves, 512, 256),
        ],
        compiler_params=pltpu.CompilerParams(vmem_limit_bytes=24 << 20),
        cost_estimate=pl.CostEstimate(flops=1_000_000, bytes_accessed=1_000, transcendentals=0),
        name="front",
    )(masks, *tops, *mids, *prepared)


def make_back_kernel(planes, leaves):
    def kernel(
        mask_ref, b0, b1, b2, b3,
        x_h, x_l, tt_h, tt_l, tl_h, tl_l, base_top, base_leaf, c_own,
        col_top, diag_top, col_mid, cross_mid, diag_mid, col_leaf, cross_c, cross_e, diag_leaf,
        blocks, a_h, a_l, cb_h, cb_l, c_s, d_s, e_s, f_s, top_s, mid_s, sem,
    ):
        device = lax.axis_index("row")
        plane = own_plane(device, planes)
        quarter = device % 4
        half = device % 2
        copies = []

        def move(src, dst):
            copy = pltpu.make_async_copy(src, dst, sem.at[len(copies)])
            copy.start()
            copies.append(copy)
            return copy

        masks = [-mask_ref[r : r + 1, :] for r in range(4)]
        for k, ref in enumerate((b0, b1, b2, b3)):
            for n in range(6):
                blocks[n, :, at((quarter ^ k) * 32, 32), :] = ref[:, n * 32 : n * 32 + 32, :]
        for n, (row, col) in enumerate(((1, 1), (1, 2), (1, 3), (2, 2), (2, 3), (3, 3))):
            re, im = blocks[n, 0], blocks[n, 1]
            put_pair(a_h, a_l, row * 128 - 128, col * 256 - 256, re, im)
            if row != col:
                put_pair(a_h, a_l, col * 128 - 128, row * 256 - 256, re.T, im.T)

        def columns(j, out):
            got = mm3(a_h[...], a_l[...], x_h[j, 256:1024], x_l[j, 256:1024])
            for r in range(4):
                rows = slice(r * 128, r * 128 + 128)
                place = at((plane ^ r) * 128, 128)
                for part in (0, 1):
                    lanes = slice(part * 128, part * 128 + 128)
                    c = c_own[j, rows, lanes]
                    if r:
                        c = c + got[r * 128 - 128 : r * 128, lanes]
                    c = c * masks[r]
                    hi, lo = halves(c)
                    cb_h[j, rows, lanes] = hi
                    cb_l[j, rows, lanes] = lo
                    out[part, place, :] = c

        def against(j, t_h, t_l):
            got = mm3(t_h, t_l, cb_h[j], cb_l[j])
            outs = []
            for n in range(t_h.shape[0] // 256):
                g = got[n * 256 : n * 256 + 256]
                outs.append((g[0:128, 0:128] - g[128:256, 128:256], g[0:128, 128:256] + g[128:256, 0:128]))
            return outs

        def leaf_tail(j):
            th = jnp.concatenate([tt_h[...], tl_h[j]], axis=0)
            tl = jnp.concatenate([tt_l[...], tl_l[j]], axis=0)
            zs = against(2 + j, th, tl)
            for n, (z, out) in enumerate(zip(zs, (e_s, d_s, f_s))):
                for part in (0, 1):
                    out[j, part] = base_leaf[j, n, part] - z[part]
            mine = slice(j * 128, j * 128 + 128)
            move(e_s.at[j], cross_e.at[:, mine, :])
            move(d_s.at[j], cross_c.at[:, mine, :])
            move(f_s.at[j], diag_leaf.at[:, mine, :])

        for j in range(leaves):
            columns(2 + j, c_s.at[2 + j])
            move(c_s.at[2 + j], col_leaf.at[:, j * 512 : j * 512 + 512, :])
        columns(1, c_s.at[1])
        move(c_s.at[1, :, at(half * 256, 256), :], col_mid)
        columns(0, c_s.at[0])
        move(c_s.at[0, :, at(quarter * 128, 128), :], col_top)
        for j in range(leaves):
            leaf_tail(j)
        zs = against(1, tt_h[...], tt_l[...])
        for n in (0, 1):
            for part in (0, 1):
                mid_s[n, part] = base_top[1 + n, part] - zs[n][part]
        move(mid_s.at[0, :, at(half * 64, 64), :], cross_mid)
        move(mid_s.at[1, :, at(half * 64, 64), :], diag_mid)
        (z,) = against(0, tt_h[0:256], tt_l[0:256])
        for part in (0, 1):
            top_s[part] = base_top[0, part] - z[part]
        move(top_s.at[:, at(quarter * 32, 32), :], diag_top)
        for copy in copies:
            copy.wait()

    return kernel


def back(planes, masks, root, firsts, leaves):
    n = leaves + 2
    v = pltpu.VMEM
    shapes = [(2, 128, 128), (2, 32, 128), (2, 256, 128), (2, 64, 128), (2, 64, 128)]
    shapes += [(2, leaves * rows, 128) for rows in (512, 128, 128, 128)]
    pair = lambda *shape: [v(shape, BF16)] * 2
    return pl.pallas_call(
        make_back_kernel(planes, leaves),
        out_shape=tuple(jax.ShapeDtypeStruct(s, F32) for s in shapes),
        in_specs=[VMEM] * (5 + len(firsts)),
        out_specs=(ANY,) * len(shapes),
        scratch_shapes=[
            v((6, 2, 128, 128), F32), *pair(384, 768), *pair(n, 512, 256), v((n, 2, 512, 128), F32),
            v((leaves, 2, 128, 128), F32), v((leaves, 2, 128, 128), F32), v((leaves, 2, 128, 128), F32),
            v((2, 128, 128), F32), v((2, 2, 128, 128), F32),
            pltpu.SemaphoreType.DMA((10 + 4 * leaves,)),
        ],
        compiler_params=pltpu.CompilerParams(vmem_limit_bytes=24 << 20),
        cost_estimate=pl.CostEstimate(flops=8_000_000_000, bytes_accessed=12_000_000, transcendentals=0),
        name="back",
    )(masks, *root, *firsts)


def root_gathered(ainv_root):
    device = lax.axis_index("row")
    full = lax.all_gather(ainv_root, "row", axis=1, tiled=True)
    quarter = device % 4
    own = lax.dynamic_slice_in_dim(full, quarter * 32, 32, 1)
    root = []
    for k in range(4):
        pieces = []
        for row, col in ((1, 1), (1, 2), (1, 3), (2, 2), (2, 3), (3, 3)):
            block = full[:, row * 128 : row * 128 + 128, col * 128 : col * 128 + 128]
            pieces.append(lax.dynamic_slice_in_dim(block, (quarter ^ k) * 32, 32, 1))
        root.append(jnp.concatenate(pieces, axis=1))
    return own, root


def local(
    ainv_root, pattern, panel_top, inv_top, panel_mid, link_mid, inv_mid,
    panel_leaf, link_leaf_mid, link_leaf_top, inv_leaf,
):
    planes = lax.axis_size("row") == 16
    leaves = panel_leaf.shape[1] // 512
    prepared = prep(panel_leaf, link_leaf_mid, link_leaf_top, inv_leaf)
    if planes:
        top, mid, masks, *sent = pack(
            pattern, ainv_root, panel_top, inv_top, panel_mid, link_mid, inv_mid
        )
        got = [swap(x, 4 * k) for k, x in zip((1, 2, 3), sent)]
        *got, top_1, mid_1 = lax.optimization_barrier((*got, top, mid, *prepared))[:5]
        far_top = swap(top, 2)
        tops = [top, swap(top_1, 1), far_top, swap(far_top, 1)]
        mids = [mid, swap(mid_1, 1)]
        near = join(*got)
        far = swap(near, 2)
        root = [near, swap(near, 1)]
    else:
        mid = jnp.concatenate([panel_mid, link_mid, inv_mid], axis=1)
        node = lax.dynamic_index_in_dim(pattern, lax.axis_index("row") // 4, 0, keepdims=False)
        masks = jnp.broadcast_to(jnp.pad(node.astype(F32), (0, 4))[:, None], (8, 128))
        own, root = root_gathered(ainv_root)
        own = [own[:, :, n * 128 : n * 128 + 128] for n in range(4)]
        top = jnp.concatenate([panel_top, inv_top, *own], axis=1)
        far_top = swap(top, 2)
        tops = [top, swap(top, 1), far_top, swap(far_top, 1)]
        mids = [mid, swap(mid, 1)]
    firsts = front(planes, masks, tops, mids, prepared)
    if planes:
        far, *firsts = lax.optimization_barrier((far, *firsts))
        root += [far, swap(far, 1)]
    return back(planes, masks, root, firsts, leaves)


def solution(mesh):
    split = P("pole", "row", None)
    return jax.shard_map(
        local,
        mesh=mesh,
        in_specs=(split, P()) + (split,) * 9,
        out_specs=(split,) * 9,
        check_vma=False,
    )
```

```python
import jax
import jax.numpy as jnp
from jax import lax
from jax.experimental import pallas as pl
from jax.experimental.pallas import tpu as pltpu
from jax.sharding import PartitionSpec as P

F32 = jnp.float32
BF16 = jnp.bfloat16
ANY = pl.BlockSpec(memory_space=pl.ANY)
VMEM = pl.BlockSpec(memory_space=pltpu.VMEM)


def swap(x, apart):
    return lax.ppermute(x, "row", [(i, i ^ apart) for i in range(lax.axis_size("row"))])


def halves(x):
    hi = x.astype(BF16)
    return hi, (x - hi.astype(F32)).astype(BF16)


def mm(a, b):
    return jnp.dot(a, b, preferred_element_type=F32)


def mm3(ah, al, bh, bl):
    return mm(ah, bh) + (mm(ah, bl) + mm(al, bh))


def at(start, size):
    return pl.ds(pl.multiple_of(start, size), size)


def in_hbm(x):
    return pltpu.with_memory_space_constraint(x, pltpu.HBM)


def own_plane(device, planes):
    return device // 4 if planes else device * 0


def pack_kernel(pat, a_hbm, t_hbm, i_hbm, pm_hbm, lm_hbm, im_hbm, top, mine, masks, z1, z2, z3, pat_s, sem):
    plane = lax.axis_index("row") // 4
    pairs = [(pat, pat_s)]
    for dst in (top, mine):
        pairs += [(t_hbm, dst.at[:, 0:128, :]), (i_hbm, dst.at[:, 128:160, :])]
        for n in range(4):
            pairs.append((a_hbm.at[:, :, n * 128 : n * 128 + 128], dst.at[:, 160 + n * 32 : 192 + n * 32, :]))
    pairs += [
        (pm_hbm, mine.at[:, 288:544, :]), (lm_hbm, mine.at[:, 544:608, :]), (im_hbm, mine.at[:, 608:672, :]),
    ]
    for dst, order in ((z1, (0, 3, 2)), (z2, (0, 1)), (z3, (0,))):
        for n, apart in enumerate(order):
            pairs.append((a_hbm.at[:, :, at((plane ^ apart) * 128, 128)], dst.at[:, n * 32 : n * 32 + 32, :]))
    copies = [pltpu.make_async_copy(src, dst, sem.at[n]) for n, (src, dst) in enumerate(pairs)]
    for copy in copies:
        copy.start()
    copies[0].wait()
    for r in range(4):
        masks[r : r + 1, :] = jnp.full((1, 128), pat_s[plane, plane ^ r], jnp.int32).astype(F32)
    masks[4:8, :] = jnp.zeros((4, 128), F32)
    for copy in copies[1:]:
        copy.wait()


def pack(pattern, *mine):
    shapes = [(2, 288, 128), (2, 672, 128), (8, 128), (2, 96, 128), (2, 64, 128), (2, 32, 128)]
    return pl.pallas_call(
        pack_kernel,
        out_shape=tuple(jax.ShapeDtypeStruct(s, F32) for s in shapes),
        in_specs=[ANY] * 7,
        out_specs=(VMEM,) * len(shapes),
        scratch_shapes=[pltpu.SMEM(pattern.shape, jnp.int32), pltpu.SemaphoreType.DMA((22,))],
        compiler_params=pltpu.CompilerParams(vmem_limit_bytes=4 << 20),
        cost_estimate=pl.CostEstimate(flops=1_000_000, bytes_accessed=1_000, transcendentals=0),
        name="pack_panels",
    )(in_hbm(pattern), *(in_hbm(x) for x in mine))


def join_kernel(z1, z2, z3, far_top, near, both):
    for ref in (near, both):
        ref[:, 0:96, :] = z1[...]
        ref[:, 96:160, :] = z2[...]
        ref[:, 160:192, :] = z3[...]
    both[:, 192:480, :] = far_top[...]


def join(*blocks):
    return pl.pallas_call(
        join_kernel,
        out_shape=(jax.ShapeDtypeStruct((2, 192, 128), F32), jax.ShapeDtypeStruct((2, 480, 128), F32)),
        in_specs=[VMEM] * 4,
        out_specs=(VMEM, VMEM),
        compiler_params=pltpu.CompilerParams(vmem_limit_bytes=4 << 20),
        cost_estimate=pl.CostEstimate(flops=1_000_000, bytes_accessed=1_000, transcendentals=0),
        name="join_root",
    )(*blocks)


def put_rhs(ref_h, ref_l, row, re, im):
    rh, rl = halves(re)
    ih, il = halves(im)
    for ref, r, i in ((ref_h, rh, ih), (ref_l, rl, il)):
        ref[row : row + 128, 0:128] = r
        ref[row : row + 128, 128:256] = i
        ref[row + 128 : row + 256, 0:128] = -i
        ref[row + 128 : row + 256, 128:256] = r


def put_pair(ref_h, ref_l, row, col, re, im):
    n = re.shape[0]
    rh, rl = halves(re)
    ih, il = halves(im)
    for ref, r, i in ((ref_h, rh, ih), (ref_l, rl, il)):
        ref[row : row + n, col : col + 128] = r
        ref[row : row + n, col + 128 : col + 256] = i


def put_transposed(ref_h, ref_l, row, r, re, im):
    for part, x in ((0, re), (128, im)):
        xh, xl = halves(x.T)
        ref_h[row + part : row + part + 128, r * 128 : r * 128 + 128] = xh
        ref_l[row + part : row + part + 128, r * 128 : r * 128 + 128] = xl


def make_prep_kernel(leaves):
    def kernel(panel, link_c, link_e, inv, g, li, rhs_h, rhs_l, auxl_h, auxl_l, lc_s, le_s, sem):
        pairs = ((link_c, lc_s), (link_e, le_s), (panel, g), (inv, li))
        copies = [pltpu.make_async_copy(src, dst, sem.at[n]) for n, (src, dst) in enumerate(pairs)]
        for copy in copies:
            copy.start()
        for row, ref, copy in ((0, lc_s, copies[0]), (256, le_s, copies[1])):
            copy.wait()
            for j in range(leaves):
                mine = slice(j * 128, j * 128 + 128)
                re, im = ref[0, mine], ref[1, mine]
                put_rhs(rhs_h.at[j], rhs_l.at[j], row, re, im)
                put_pair(auxl_h.at[j], auxl_l.at[j], 0, row, re.T, im.T)
        copies[2].wait()
        copies[3].wait()

    return kernel


def prep(panel, link_c, link_e, inv):
    leaves = panel.shape[1] // 512
    v = pltpu.VMEM
    out = [(panel.shape, F32), (inv.shape, F32)]
    out += [((leaves, 512, 256), BF16)] * 2 + [((leaves, 128, 512), BF16)] * 2
    return pl.pallas_call(
        make_prep_kernel(leaves),
        out_shape=tuple(jax.ShapeDtypeStruct(s, d) for s, d in out),
        in_specs=[ANY] * 4,
        out_specs=(VMEM,) * len(out),
        scratch_shapes=[v(link_c.shape, F32), v(link_e.shape, F32), pltpu.SemaphoreType.DMA((4,))],
        compiler_params=pltpu.CompilerParams(vmem_limit_bytes=12 << 20),
        cost_estimate=pl.CostEstimate(flops=1_000_000, bytes_accessed=1_000, transcendentals=0),
        name="prep",
    )(in_hbm(panel), in_hbm(link_c), in_hbm(link_e), in_hbm(inv))


def own_columns(j, row_h, row_l, col_h, col_l, x_h, x_l, out, first=0):
    out[j - first, 0:128] = mm3(row_h[...], row_l[...], x_h[j], x_l[j])
    out[j - first, 128:512] = mm3(col_h[...], col_l[...], x_h[j, 0:256], x_l[j, 0:256])


def make_front_kernel(planes, leaves):
    def kernel(
        mask_ref, mine, other, both, both_other, g_s, li_s, rhs_h, rhs_l, auxl_h, auxl_l,
        x_h, x_l, tt_h, tt_l, tl_h, tl_l, base_top, base_leaf, row_h, row_l, col_h, col_l, c_top,
        l_s, b_s, t0_s, am_s, d_s, own,
        lhs_h, lhs_l, ra_h, ra_l, rq_h, rq_l, aux_h, aux_l, rrs_h, rrs_l,
    ):
        device = lax.axis_index("row")
        plane = own_plane(device, planes)
        quarter = device % 4
        half = device % 2
        def rel(supernode):
            return at((supernode ^ plane) * 128, 128)

        for k, (ref, row) in enumerate(((mine, 0), (other, 0), (both, 192), (both_other, 192))):
            q = quarter ^ k
            l_s[:, rel(q), :] = ref[:, row : row + 128, :]
            t0_s[:, at(q * 32, 32), :] = ref[:, row + 128 : row + 160, :]
            for n in range(4):
                own[:, at(q * 32, 32), n * 128 : n * 128 + 128] = (
                    ref[:, row + 160 + n * 32 : row + 192 + n * 32, :]
                )
        for k, ref in enumerate((mine, other)):
            h = half ^ k
            for n in (0, 1):
                b_s[:, rel(h * 2 + n), :] = ref[:, 288 + n * 128 : 416 + n * 128, :]
            am_s[:, at(h * 64, 64), :] = ref[:, 544:608, :]
            d_s[:, at(h * 64, 64), :] = ref[:, 608:672, :]
        masks = [mask_ref[r : r + 1, :] for r in range(4)]

        def put_x(j, r, re, im):
            put_rhs(x_h.at[j], x_l.at[j], r * 256, re, im)

        put_rhs(ra_h, ra_l, 0, am_s[0], am_s[1])
        for r in range(4):
            rows = slice(r * 128, r * 128 + 128)
            re, im = l_s[0, rows] * masks[r], l_s[1, rows] * masks[r]
            put_pair(lhs_h, lhs_l, r * 128, 256, re, im)
            put_x(0, r, re, im)
            put_transposed(tt_h, tt_l, 0, r, re, im)
        put_pair(lhs_h, lhs_l, 640, 256, t0_s[0], t0_s[1])
        ah, al = ra_h[...], ra_l[...]
        got = mm3(lhs_h[0:512, 256:512], lhs_l[0:512, 256:512], ah, al)
        for r in range(4):
            rows = slice(r * 128, r * 128 + 128)
            re = b_s[0, rows] * masks[r] - got[rows, 0:128]
            im = b_s[1, rows] * masks[r] - got[rows, 128:256]
            put_pair(lhs_h, lhs_l, r * 128, 0, re, im)
            put_x(1, r, re, im)
            put_transposed(tt_h, tt_l, 256, r, re, im)
        got = mm3(lhs_h[640:768, 256:512], lhs_l[640:768, 256:512], ah, al)
        q_r, q_i = -got[:, 0:128], -got[:, 128:256]
        put_pair(lhs_h, lhs_l, 640, 0, q_r, q_i)
        put_pair(lhs_h, lhs_l, 512, 256, q_r.T, q_i.T)
        put_rhs(rq_h, rq_l, 0, q_r, q_i)
        put_pair(aux_h, aux_l, 0, 0, am_s[0].T, am_s[1].T)
        got = mm3(aux_h[...], aux_l[...], rq_h[...], rq_l[...])
        d_r, d_i = d_s[0] - got[:, 0:128], d_s[1] - got[:, 128:256]
        put_pair(lhs_h, lhs_l, 512, 0, d_r, d_i)
        base_top[0] = t0_s[...]
        base_top[1, 0] = q_r
        base_top[1, 1] = q_i
        base_top[2, 0] = d_r
        base_top[2, 1] = d_i

        for r in range(4):
            cols = at((plane ^ r) * 128, 128)
            re, im = own[0, :, cols], own[1, :, cols]
            put_pair(row_h, row_l, 0, r * 256, re, im)
            if r:
                put_pair(col_h, col_l, (r - 1) * 128, 0, re.T, im.T)
        for j in (0, 1):
            own_columns(j, row_h, row_l, col_h, col_l, x_h, x_l, c_top)
        for j in range(leaves):
            got = mm3(lhs_h[...], lhs_l[...], rhs_h[j], rhs_l[j])
            for r in range(4):
                rows = slice(r * 128, r * 128 + 128)
                mine = at(j * 512 + (plane ^ r) * 128, 128)
                re = g_s[0, mine] * masks[r] - got[rows, 0:128]
                im = g_s[1, mine] * masks[r] - got[rows, 128:256]
                put_x(2 + j, r, re, im)
                put_transposed(tl_h.at[j], tl_l.at[j], 0, r, re, im)
            r_r, r_i = -got[512:640, 0:128], -got[512:640, 128:256]
            s_r, s_i = -got[640:768, 0:128], -got[640:768, 128:256]
            put_rhs(rrs_h.at[j], rrs_l.at[j], 0, r_r, r_i)
            put_rhs(rrs_h.at[j], rrs_l.at[j], 256, s_r, s_i)
            base_leaf[j, 0, 0] = s_r
            base_leaf[j, 0, 1] = s_i
            base_leaf[j, 1, 0] = r_r
            base_leaf[j, 1, 1] = r_i
        for j in range(leaves):
            mine = slice(j * 128, j * 128 + 128)
            got = mm3(auxl_h[j], auxl_l[j], rrs_h[j], rrs_l[j])
            base_leaf[j, 2, 0] = li_s[0, mine] - got[:, 0:128]
            base_leaf[j, 2, 1] = li_s[1, mine] - got[:, 128:256]

    return kernel


def front(planes, masks, pieces, prepared):
    leaves = prepared[0].shape[1] // 512
    n = leaves + 2
    v = pltpu.VMEM
    out = [
        ((n, 1024, 256), BF16), ((n, 1024, 256), BF16), ((512, 512), BF16), ((512, 512), BF16),
        ((leaves, 256, 512), BF16), ((leaves, 256, 512), BF16),
        ((3, 2, 128, 128), F32), ((leaves, 3, 2, 128, 128), F32),
        ((128, 1024), BF16), ((128, 1024), BF16), ((384, 256), BF16), ((384, 256), BF16),
        ((2, 512, 256), F32),
    ]
    pair = lambda *shape: [v(shape, BF16)] * 2
    return pl.pallas_call(
        make_front_kernel(planes, leaves),
        out_shape=tuple(jax.ShapeDtypeStruct(s, d) for s, d in out),
        in_specs=[VMEM] * 11,
        out_specs=(VMEM,) * len(out),
        scratch_shapes=[
            v((2, 512, 128), F32), v((2, 512, 128), F32),
            v((2, 128, 128), F32), v((2, 128, 128), F32), v((2, 128, 128), F32),
            v((2, 128, 512), F32), *pair(768, 512), *pair(256, 256), *pair(256, 256), *pair(128, 256),
            *pair(leaves, 512, 256),
        ],
        compiler_params=pltpu.CompilerParams(vmem_limit_bytes=24 << 20),
        cost_estimate=pl.CostEstimate(flops=1_000_000, bytes_accessed=1_000, transcendentals=0),
        name="front",
    )(masks, *pieces, *prepared)


def own_kernel(row_h, row_l, col_h, col_l, x_h, x_l, c_leaf):
    for j in range(2, x_h.shape[0]):
        own_columns(j, row_h, row_l, col_h, col_l, x_h, x_l, c_leaf, 2)


def own_product(row_h, row_l, col_h, col_l, x_h, x_l):
    return pl.pallas_call(
        own_kernel,
        out_shape=jax.ShapeDtypeStruct((x_h.shape[0] - 2, 512, 256), F32),
        in_specs=[VMEM] * 6,
        out_specs=VMEM,
        compiler_params=pltpu.CompilerParams(vmem_limit_bytes=12 << 20),
        cost_estimate=pl.CostEstimate(flops=1_000_000, bytes_accessed=1_000, transcendentals=0),
        name="own_product",
    )(row_h, row_l, col_h, col_l, x_h, x_l)


def make_back_kernel(planes, leaves):
    def kernel(
        mask_ref, b0, b1, b2, b3,
        x_h, x_l, tt_h, tt_l, tl_h, tl_l, base_top, base_leaf, c_top, c_leaf,
        col_top, diag_top, col_mid, cross_mid, diag_mid, col_leaf, cross_c, cross_e, diag_leaf,
        blocks, a_h, a_l, cb_h, cb_l, c_s, d_s, e_s, f_s, top_s, mid_s, sem,
    ):
        device = lax.axis_index("row")
        plane = own_plane(device, planes)
        quarter = device % 4
        half = device % 2
        copies = []

        def move(src, dst):
            copy = pltpu.make_async_copy(src, dst, sem.at[len(copies)])
            copy.start()
            copies.append(copy)
            return copy

        masks = [-mask_ref[r : r + 1, :] for r in range(4)]
        for k, ref in enumerate((b0, b1, b2, b3)):
            for n in range(6):
                blocks[n, :, at((quarter ^ k) * 32, 32), :] = ref[:, n * 32 : n * 32 + 32, :]
        for n, (row, col) in enumerate(((1, 1), (1, 2), (1, 3), (2, 2), (2, 3), (3, 3))):
            re, im = blocks[n, 0], blocks[n, 1]
            put_pair(a_h, a_l, row * 128 - 128, col * 256 - 256, re, im)
            if row != col:
                put_pair(a_h, a_l, col * 128 - 128, row * 256 - 256, re.T, im.T)

        def columns(j, out):
            got = mm3(a_h[...], a_l[...], x_h[j, 256:1024], x_l[j, 256:1024])
            for r in range(4):
                rows = slice(r * 128, r * 128 + 128)
                place = at((plane ^ r) * 128, 128)
                for part in (0, 1):
                    lanes = slice(part * 128, part * 128 + 128)
                    c = c_leaf[j - 2, rows, lanes] if j > 1 else c_top[j, rows, lanes]
                    if r:
                        c = c + got[r * 128 - 128 : r * 128, lanes]
                    c = c * masks[r]
                    hi, lo = halves(c)
                    cb_h[j, rows, lanes] = hi
                    cb_l[j, rows, lanes] = lo
                    out[part, place, :] = c

        def against(j, t_h, t_l):
            got = mm3(t_h, t_l, cb_h[j], cb_l[j])
            outs = []
            for n in range(t_h.shape[0] // 256):
                g = got[n * 256 : n * 256 + 256]
                outs.append((g[0:128, 0:128] - g[128:256, 128:256], g[0:128, 128:256] + g[128:256, 0:128]))
            return outs

        def leaf_tail(j):
            th = jnp.concatenate([tt_h[...], tl_h[j]], axis=0)
            tl = jnp.concatenate([tt_l[...], tl_l[j]], axis=0)
            zs = against(2 + j, th, tl)
            for n, (z, out) in enumerate(zip(zs, (e_s, d_s, f_s))):
                for part in (0, 1):
                    out[j, part] = base_leaf[j, n, part] - z[part]
            mine = slice(j * 128, j * 128 + 128)
            move(e_s.at[j], cross_e.at[:, mine, :])
            move(d_s.at[j], cross_c.at[:, mine, :])
            move(f_s.at[j], diag_leaf.at[:, mine, :])

        for j in range(leaves):
            columns(2 + j, c_s.at[2 + j])
            move(c_s.at[2 + j], col_leaf.at[:, j * 512 : j * 512 + 512, :])
        columns(1, c_s.at[1])
        move(c_s.at[1, :, at(half * 256, 256), :], col_mid)
        columns(0, c_s.at[0])
        move(c_s.at[0, :, at(quarter * 128, 128), :], col_top)
        for j in range(leaves):
            leaf_tail(j)
        zs = against(1, tt_h[...], tt_l[...])
        for n in (0, 1):
            for part in (0, 1):
                mid_s[n, part] = base_top[1 + n, part] - zs[n][part]
        move(mid_s.at[0, :, at(half * 64, 64), :], cross_mid)
        move(mid_s.at[1, :, at(half * 64, 64), :], diag_mid)
        (z,) = against(0, tt_h[0:256], tt_l[0:256])
        for part in (0, 1):
            top_s[part] = base_top[0, part] - z[part]
        move(top_s.at[:, at(quarter * 32, 32), :], diag_top)
        for copy in copies:
            copy.wait()

    return kernel


def back(planes, masks, root, firsts, leaves):
    n = leaves + 2
    v = pltpu.VMEM
    shapes = [(2, 128, 128), (2, 32, 128), (2, 256, 128), (2, 64, 128), (2, 64, 128)]
    shapes += [(2, leaves * rows, 128) for rows in (512, 128, 128, 128)]
    pair = lambda *shape: [v(shape, BF16)] * 2
    return pl.pallas_call(
        make_back_kernel(planes, leaves),
        out_shape=tuple(jax.ShapeDtypeStruct(s, F32) for s in shapes),
        in_specs=[VMEM] * (5 + len(firsts)),
        out_specs=(ANY,) * len(shapes),
        scratch_shapes=[
            v((6, 2, 128, 128), F32), *pair(384, 768), *pair(n, 512, 256), v((n, 2, 512, 128), F32),
            v((leaves, 2, 128, 128), F32), v((leaves, 2, 128, 128), F32), v((leaves, 2, 128, 128), F32),
            v((2, 128, 128), F32), v((2, 2, 128, 128), F32),
            pltpu.SemaphoreType.DMA((10 + 4 * leaves,)),
        ],
        compiler_params=pltpu.CompilerParams(vmem_limit_bytes=24 << 20),
        cost_estimate=pl.CostEstimate(flops=8_000_000_000, bytes_accessed=12_000_000, transcendentals=0),
        name="back",
    )(masks, *root, *firsts)


def root_gathered(ainv_root):
    device = lax.axis_index("row")
    full = lax.all_gather(ainv_root, "row", axis=1, tiled=True)
    quarter = device % 4
    own = lax.dynamic_slice_in_dim(full, quarter * 32, 32, 1)
    root = []
    for k in range(4):
        pieces = []
        for row, col in ((1, 1), (1, 2), (1, 3), (2, 2), (2, 3), (3, 3)):
            block = full[:, row * 128 : row * 128 + 128, col * 128 : col * 128 + 128]
            pieces.append(lax.dynamic_slice_in_dim(block, (quarter ^ k) * 32, 32, 1))
        root.append(jnp.concatenate(pieces, axis=1))
    return own, root


def local(
    ainv_root, pattern, panel_top, inv_top, panel_mid, link_mid, inv_mid,
    panel_leaf, link_leaf_mid, link_leaf_top, inv_leaf,
):
    planes = lax.axis_size("row") == 16
    leaves = panel_leaf.shape[1] // 512
    prepared = prep(panel_leaf, link_leaf_mid, link_leaf_top, inv_leaf)
    if planes:
        top, mine, masks, *sent = pack(
            pattern, ainv_root, panel_top, inv_top, panel_mid, link_mid, inv_mid
        )
        got = [swap(x, 4 * k) for k, x in zip((1, 2, 3), sent)]
        *got, _ = lax.optimization_barrier((*got, *prepared))[:4]
        near, both = join(*got, swap(top, 2))
        far = swap(near, 2)
    else:
        node = lax.dynamic_index_in_dim(pattern, lax.axis_index("row") // 4, 0, keepdims=False)
        masks = jnp.broadcast_to(jnp.pad(node.astype(F32), (0, 4))[:, None], (8, 128))
        own, root = root_gathered(ainv_root)
        own = [own[:, :, n * 128 : n * 128 + 128] for n in range(4)]
        top = jnp.concatenate([panel_top, inv_top, *own], axis=1)
        mine = jnp.concatenate([top, panel_mid, link_mid, inv_mid], axis=1)
        both = jnp.concatenate([root[0], swap(top, 2)], axis=1)
    pieces = [mine, swap(mine, 1), both, swap(both, 1)]
    firsts = front(planes, masks, pieces, prepared)
    if planes:
        far, *firsts = lax.optimization_barrier((far, *firsts))
        root = [both, pieces[3], far, swap(far, 1)]
    c_leaf = own_product(*firsts[8:12], *firsts[:2])
    return back(planes, masks, root, [*firsts[:8], firsts[12], c_leaf], leaves)


def solution(mesh):
    split = P("pole", "row", None)
    return jax.shard_map(
        local,
        mesh=mesh,
        in_specs=(split, P()) + (split,) * 9,
        out_specs=(split,) * 9,
        check_vma=False,
    )
```

```python
import jax
import jax.numpy as jnp
from jax import lax
from jax.experimental import pallas as pl
from jax.experimental.pallas import tpu as pltpu
from jax.sharding import PartitionSpec as P

F32 = jnp.float32
BF16 = jnp.bfloat16
ANY = pl.BlockSpec(memory_space=pl.ANY)
VMEM = pl.BlockSpec(memory_space=pltpu.VMEM)


def swap(x, apart):
    return lax.ppermute(x, "row", [(i, i ^ apart) for i in range(lax.axis_size("row"))])


def halves(x):
    hi = x.astype(BF16)
    return hi, (x - hi.astype(F32)).astype(BF16)


def mm(a, b):
    return jnp.dot(a, b, preferred_element_type=F32)


def mm3(ah, al, bh, bl):
    return mm(ah, bh) + (mm(ah, bl) + mm(al, bh))


def at(start, size):
    return pl.ds(pl.multiple_of(start, size), size)


def in_hbm(x):
    return pltpu.with_memory_space_constraint(x, pltpu.HBM)


def own_plane(device, planes):
    return device // 4 if planes else device * 0


def pack_kernel(
    pat, a_hbm, t_hbm, i_hbm, pm_hbm, lm_hbm, im_hbm, top, mine, masks, z1, z2, z3, a, pat_s, sem
):
    plane = lax.axis_index("row") // 4
    pairs = (
        (a_hbm, a), (t_hbm, mine.at[:, 0:128, :]), (i_hbm, mine.at[:, 128:160, :]), (pat, pat_s),
        (pm_hbm, mine.at[:, 288:544, :]), (lm_hbm, mine.at[:, 544:608, :]), (im_hbm, mine.at[:, 608:672, :]),
    )
    copies = [pltpu.make_async_copy(src, dst, sem.at[n]) for n, (src, dst) in enumerate(pairs)]
    for copy in copies:
        copy.start()
    copies[0].wait()
    for dst in (top, mine):
        for n in range(4):
            dst[:, 160 + n * 32 : 192 + n * 32, :] = a[:, :, n * 128 : n * 128 + 128]
    for dst, order in ((z1, (0, 3, 2)), (z2, (0,)), (z3, (0, 1))):
        for n, apart in enumerate(order):
            dst[:, n * 32 : n * 32 + 32, :] = a[:, :, at((plane ^ apart) * 128, 128)]
    copies[1].wait()
    copies[2].wait()
    top[:, 0:160, :] = mine[:, 0:160, :]
    copies[3].wait()
    for r in range(4):
        masks[r : r + 1, :] = jnp.full((1, 128), pat_s[plane, plane ^ r], jnp.int32).astype(F32)
    masks[4:8, :] = jnp.zeros((4, 128), F32)
    for copy in copies[4:]:
        copy.wait()


def pack(pattern, *mine):
    shapes = [(2, 288, 128), (2, 672, 128), (8, 128), (2, 96, 128), (2, 32, 128), (2, 64, 128)]
    return pl.pallas_call(
        pack_kernel,
        out_shape=tuple(jax.ShapeDtypeStruct(s, F32) for s in shapes),
        in_specs=[ANY] * 7,
        out_specs=(VMEM,) * len(shapes),
        scratch_shapes=[
            pltpu.VMEM(mine[0].shape, F32), pltpu.SMEM(pattern.shape, jnp.int32), pltpu.SemaphoreType.DMA((7,)),
        ],
        compiler_params=pltpu.CompilerParams(vmem_limit_bytes=4 << 20),
        cost_estimate=pl.CostEstimate(flops=1_000_000, bytes_accessed=1_000, transcendentals=0),
        name="pack_panels",
    )(in_hbm(pattern), *(in_hbm(x) for x in mine))


def join_kernel(z1, z2, z3, far_top, lead, rest, both):
    plane = lax.axis_index("row") // 4
    for n, apart in enumerate((0, 3, 2)):
        lead[:, n * 32 : n * 32 + 32, :] = far_top[:, at(160 + (plane ^ apart) * 32, 32), :]
    rest[:, 0:32, :] = z2[...]
    rest[:, 32:96, :] = z3[...]
    both[:, 0:96, :] = z1[...]
    both[:, 96:128, :] = z2[...]
    both[:, 128:192, :] = z3[...]
    both[:, 192:480, :] = far_top[...]


def join(*blocks):
    return pl.pallas_call(
        join_kernel,
        out_shape=tuple(jax.ShapeDtypeStruct((2, rows, 128), F32) for rows in (96, 96, 480)),
        in_specs=[VMEM] * 4,
        out_specs=(VMEM,) * 3,
        compiler_params=pltpu.CompilerParams(vmem_limit_bytes=4 << 20),
        cost_estimate=pl.CostEstimate(flops=1_000_000, bytes_accessed=1_000, transcendentals=0),
        name="join_root",
    )(*blocks)


def stack_kernel(upper, lower, joined):
    joined[:, 0:96, :] = upper[...]
    joined[:, 96:192, :] = lower[...]


def stack(upper, lower):
    return pl.pallas_call(
        stack_kernel,
        out_shape=jax.ShapeDtypeStruct((2, 192, 128), F32),
        in_specs=[VMEM] * 2,
        out_specs=VMEM,
        compiler_params=pltpu.CompilerParams(vmem_limit_bytes=4 << 20),
        cost_estimate=pl.CostEstimate(flops=1_000_000, bytes_accessed=1_000, transcendentals=0),
        name="stack_root",
    )(upper, lower)


def put_rhs(ref_h, ref_l, row, re, im):
    rh, rl = halves(re)
    ih, il = halves(im)
    for ref, r, i in ((ref_h, rh, ih), (ref_l, rl, il)):
        ref[row : row + 128, 0:128] = r
        ref[row : row + 128, 128:256] = i
        ref[row + 128 : row + 256, 0:128] = -i
        ref[row + 128 : row + 256, 128:256] = r


def put_pair(ref_h, ref_l, row, col, re, im):
    n = re.shape[0]
    rh, rl = halves(re)
    ih, il = halves(im)
    for ref, r, i in ((ref_h, rh, ih), (ref_l, rl, il)):
        ref[row : row + n, col : col + 128] = r
        ref[row : row + n, col + 128 : col + 256] = i


def put_transposed(ref_h, ref_l, row, r, re, im):
    for part, x in ((0, re), (128, im)):
        xh, xl = halves(x.T)
        ref_h[row + part : row + part + 128, r * 128 : r * 128 + 128] = xh
        ref_l[row + part : row + part + 128, r * 128 : r * 128 + 128] = xl


def make_prep_kernel(leaves):
    def kernel(panel, link_c, link_e, inv, g, li, rhs_h, rhs_l, auxl_h, auxl_l, lc_s, le_s, sem):
        pairs = ((link_c, lc_s), (link_e, le_s), (panel, g), (inv, li))
        copies = [pltpu.make_async_copy(src, dst, sem.at[n]) for n, (src, dst) in enumerate(pairs)]
        for copy in copies:
            copy.start()
        for row, ref, copy in ((0, lc_s, copies[0]), (256, le_s, copies[1])):
            copy.wait()
            for j in range(leaves):
                mine = slice(j * 128, j * 128 + 128)
                re, im = ref[0, mine], ref[1, mine]
                put_rhs(rhs_h.at[j], rhs_l.at[j], row, re, im)
                put_pair(auxl_h.at[j], auxl_l.at[j], 0, row, re.T, im.T)
        copies[2].wait()
        copies[3].wait()

    return kernel


def prep(panel, link_c, link_e, inv):
    leaves = panel.shape[1] // 512
    v = pltpu.VMEM
    out = [(panel.shape, F32), (inv.shape, F32)]
    out += [((leaves, 512, 256), BF16)] * 2 + [((leaves, 128, 512), BF16)] * 2
    return pl.pallas_call(
        make_prep_kernel(leaves),
        out_shape=tuple(jax.ShapeDtypeStruct(s, d) for s, d in out),
        in_specs=[ANY] * 4,
        out_specs=(VMEM,) * len(out),
        scratch_shapes=[v(link_c.shape, F32), v(link_e.shape, F32), pltpu.SemaphoreType.DMA((4,))],
        compiler_params=pltpu.CompilerParams(vmem_limit_bytes=12 << 20),
        cost_estimate=pl.CostEstimate(flops=1_000_000, bytes_accessed=1_000, transcendentals=0),
        name="prep",
    )(in_hbm(panel), in_hbm(link_c), in_hbm(link_e), in_hbm(inv))


def put_block(x_h, x_l, t_h, t_l, row, e, re, im):
    put_rhs(x_h, x_l, e * 256, re, im)
    put_transposed(t_h, t_l, row, e, re, im)


def places(planes):
    device = lax.axis_index("row")
    plane = own_plane(device, planes)
    shift = plane ^ (device % 4)
    return plane, shift // 2, shift % 2 == 1


def mid_blocks(planes, mine, other, b_s, am_s, ra_h, ra_l):
    plane = places(planes)[0]
    half = lax.axis_index("row") % 2
    for k, ref in enumerate((mine, other)):
        h = half ^ k
        for n in (0, 1):
            place = at(((h * 2 + n) ^ plane) * 128, 128)
            b_s[:, place, :] = ref[:, 288 + n * 128 : 416 + n * 128, :]
        am_s[:, at(h * 64, 64), :] = ref[:, 544:608, :]
    put_rhs(ra_h, ra_l, 0, am_s[0], am_s[1])


def top_block(e, swapped, first, second, row, mask):
    left, right = (second, first) if e == 0 else (first, second)
    return tuple(
        jnp.where(swapped, left[part, row : row + 128], right[part, row : row + 128]) * mask for part in (0, 1)
    )


def mid_block(block, mask, b_s, got):
    rows = at(block * 128, 128)
    return tuple(b_s[part, rows] * mask - got[:, part * 128 : part * 128 + 128] for part in (0, 1))


def leaf_block(j, supernode, mask, g, got):
    rows = at(j * 512 + supernode * 128, 128)
    return tuple(g[part, rows] * mask - got[:, part * 128 : part * 128 + 128] for part in (0, 1))


def make_head_kernel(planes):
    def kernel(
        mask_ref, mine, other, g, rhs_h, rhs_l, x_h, x_l, t_h, t_l, tl_h, tl_l,
        b_s, am_s, ra_h, ra_l, lhs_h, lhs_l,
    ):
        plane, pair, swapped = places(planes)
        mid_blocks(planes, mine, other, b_s, am_s, ra_h, ra_l)
        masks = [mask_ref[pl.ds(pair * 2 + e, 1), :] for e in (0, 1)]
        for e in (0, 1):
            re, im = top_block(e, swapped, mine, other, 0, masks[e])
            put_pair(lhs_h, lhs_l, e * 128, 256, re, im)
            put_block(x_h.at[0], x_l.at[0], t_h, t_l, 0, e, re, im)
        got = mm3(lhs_h[:, 256:512], lhs_l[:, 256:512], ra_h[...], ra_l[...])
        for e in (0, 1):
            re, im = mid_block(pair * 2 + e, masks[e], b_s, got[e * 128 : e * 128 + 128])
            put_pair(lhs_h, lhs_l, e * 128, 0, re, im)
            put_block(x_h.at[1], x_l.at[1], t_h, t_l, 256, e, re, im)
        for j in range(x_h.shape[0] - 2):
            got = mm3(lhs_h[...], lhs_l[...], rhs_h[j], rhs_l[j])
            for e in (0, 1):
                supernode = plane ^ (pair * 2 + e)
                re, im = leaf_block(j, supernode, masks[e], g, got[e * 128 : e * 128 + 128])
                put_block(x_h.at[2 + j], x_l.at[2 + j], tl_h.at[j], tl_l.at[j], 0, e, re, im)

    return kernel


def head(planes, masks, mine, other, prepared):
    g, _, rhs_h, rhs_l, _, _ = prepared
    leaves = g.shape[1] // 512
    v = pltpu.VMEM
    pair = lambda *shape: [v(shape, BF16)] * 2
    shapes = [(leaves + 2, 512, 256)] * 2 + [(512, 256)] * 2 + [(leaves, 256, 256)] * 2
    return pl.pallas_call(
        make_head_kernel(planes),
        out_shape=tuple(jax.ShapeDtypeStruct(s, BF16) for s in shapes),
        in_specs=[VMEM] * 6,
        out_specs=(VMEM,) * 6,
        scratch_shapes=[
            v((2, 512, 128), F32), v((2, 128, 128), F32), *pair(256, 256), *pair(256, 512),
        ],
        compiler_params=pltpu.CompilerParams(vmem_limit_bytes=16 << 20),
        cost_estimate=pl.CostEstimate(flops=1_000_000, bytes_accessed=1_000, transcendentals=0),
        name="head",
    )(masks, mine, other, g, rhs_h, rhs_l)


def pick(near, r, first, second, j):
    rows = slice(r % 2 * 256, r % 2 * 256 + 256)
    if r < 2:
        return jnp.where(near, first[j, rows], second[j, rows])
    return jnp.where(near, second[j, rows], first[j, rows])


def own_columns(j, row_h, row_l, col_h, col_l, xs, out, first, planes):
    near = places(planes)[1] == 0
    xa_h, xa_l, xb_h, xb_l = xs
    xh = jnp.concatenate([xa_h[j], xb_h[j]], axis=0)
    xl = jnp.concatenate([xa_l[j], xb_l[j]], axis=0)
    out[j - first, 0:128] = mm3(row_h[...], row_l[...], xh, xl)
    out[j - first, 128:512] = mm3(
        col_h[...], col_l[...], pick(near, 0, xa_h, xb_h, j), pick(near, 0, xa_l, xb_l, j)
    )


def make_front_kernel(planes, leaves):
    def kernel(
        mask_ref, mine, other, both, both_other, g_s, li_s, rhs_h, rhs_l, auxl_h, auxl_l, xa_h, xa_l,
        x_h, x_l, t_h, t_l, tl_h, tl_l, base_top, base_leaf, row_h, row_l, col_h, col_l, c_top,
        b_s, t0_s, am_s, d_s, own,
        lhs_h, lhs_l, ra_h, ra_l, rq_h, rq_l, aux_h, aux_l, rrs_h, rrs_l,
    ):
        device = lax.axis_index("row")
        plane = own_plane(device, planes)
        quarter = device % 4
        half = device % 2
        for k, (ref, row) in enumerate(((mine, 0), (other, 0), (both, 192), (both_other, 192))):
            q = quarter ^ k
            t0_s[:, at(q * 32, 32), :] = ref[:, row + 128 : row + 160, :]
            for n in range(4):
                own[:, at(q * 32, 32), n * 128 : n * 128 + 128] = (
                    ref[:, row + 160 + n * 32 : row + 192 + n * 32, :]
                )
        for k, ref in enumerate((mine, other)):
            d_s[:, at((half ^ k) * 64, 64), :] = ref[:, 608:672, :]
        mid_blocks(planes, mine, other, b_s, am_s, ra_h, ra_l)
        _, pair, swapped = places(planes)
        pair = 1 - pair
        masks = [mask_ref[pl.ds(pair * 2 + e, 1), :] for e in (0, 1)]
        for e in (0, 1):
            re, im = top_block(e, swapped, both, both_other, 192, masks[e])
            put_pair(lhs_h, lhs_l, e * 128, 256, re, im)
            put_block(x_h.at[0], x_l.at[0], t_h, t_l, 0, e, re, im)
        put_pair(lhs_h, lhs_l, 384, 256, t0_s[0], t0_s[1])
        ah, al = ra_h[...], ra_l[...]
        got = mm3(lhs_h[0:256, 256:512], lhs_l[0:256, 256:512], ah, al)
        for e in (0, 1):
            re, im = mid_block(pair * 2 + e, masks[e], b_s, got[e * 128 : e * 128 + 128])
            put_pair(lhs_h, lhs_l, e * 128, 0, re, im)
            put_block(x_h.at[1], x_l.at[1], t_h, t_l, 256, e, re, im)
        got = mm3(lhs_h[384:512, 256:512], lhs_l[384:512, 256:512], ah, al)
        q_r, q_i = -got[:, 0:128], -got[:, 128:256]
        put_pair(lhs_h, lhs_l, 384, 0, q_r, q_i)
        put_pair(lhs_h, lhs_l, 256, 256, q_r.T, q_i.T)
        put_rhs(rq_h, rq_l, 0, q_r, q_i)
        put_pair(aux_h, aux_l, 0, 0, am_s[0].T, am_s[1].T)
        got = mm3(aux_h[...], aux_l[...], rq_h[...], rq_l[...])
        d_r, d_i = d_s[0] - got[:, 0:128], d_s[1] - got[:, 128:256]
        put_pair(lhs_h, lhs_l, 256, 0, d_r, d_i)
        base_top[0] = t0_s[...]
        base_top[1, 0] = q_r
        base_top[1, 1] = q_i
        base_top[2, 0] = d_r
        base_top[2, 1] = d_i
        for n in range(4):
            cols = at((plane ^ (2 - pair * 2) ^ n) * 128, 128)
            put_pair(row_h, row_l, 0, n * 256, own[0, :, cols], own[1, :, cols])
        for r in range(1, 4):
            cols = at((plane ^ r) * 128, 128)
            put_pair(col_h, col_l, (r - 1) * 128, 0, own[0, :, cols].T, own[1, :, cols].T)
        for j in (0, 1):
            own_columns(j, row_h, row_l, col_h, col_l, (xa_h, xa_l, x_h, x_l), c_top, 0, planes)
        for j in range(leaves):
            got = mm3(lhs_h[...], lhs_l[...], rhs_h[j], rhs_l[j])
            for e in (0, 1):
                re, im = leaf_block(j, plane ^ (pair * 2 + e), masks[e], g_s, got[e * 128 : e * 128 + 128])
                put_block(x_h.at[2 + j], x_l.at[2 + j], tl_h.at[j], tl_l.at[j], 0, e, re, im)
            r_r, r_i = -got[256:384, 0:128], -got[256:384, 128:256]
            s_r, s_i = -got[384:512, 0:128], -got[384:512, 128:256]
            put_rhs(rrs_h.at[j], rrs_l.at[j], 0, r_r, r_i)
            put_rhs(rrs_h.at[j], rrs_l.at[j], 256, s_r, s_i)
            base_leaf[j, 0, 0] = s_r
            base_leaf[j, 0, 1] = s_i
            base_leaf[j, 1, 0] = r_r
            base_leaf[j, 1, 1] = r_i
        for j in range(leaves):
            mine_rows = slice(j * 128, j * 128 + 128)
            got = mm3(auxl_h[j], auxl_l[j], rrs_h[j], rrs_l[j])
            base_leaf[j, 2, 0] = li_s[0, mine_rows] - got[:, 0:128]
            base_leaf[j, 2, 1] = li_s[1, mine_rows] - got[:, 128:256]

    return kernel


def front(planes, masks, pieces, prepared, heads):
    leaves = prepared[0].shape[1] // 512
    n = leaves + 2
    v = pltpu.VMEM
    out = [
        ((n, 512, 256), BF16), ((n, 512, 256), BF16), ((512, 256), BF16), ((512, 256), BF16),
        ((leaves, 256, 256), BF16), ((leaves, 256, 256), BF16),
        ((3, 2, 128, 128), F32), ((leaves, 3, 2, 128, 128), F32),
        ((128, 1024), BF16), ((128, 1024), BF16), ((384, 256), BF16), ((384, 256), BF16),
        ((2, 512, 256), F32),
    ]
    pair = lambda *shape: [v(shape, BF16)] * 2
    return pl.pallas_call(
        make_front_kernel(planes, leaves),
        out_shape=tuple(jax.ShapeDtypeStruct(s, d) for s, d in out),
        in_specs=[VMEM] * 13,
        out_specs=(VMEM,) * len(out),
        scratch_shapes=[
            v((2, 512, 128), F32),
            v((2, 128, 128), F32), v((2, 128, 128), F32), v((2, 128, 128), F32),
            v((2, 128, 512), F32), *pair(512, 512), *pair(256, 256), *pair(256, 256), *pair(128, 256),
            *pair(leaves, 512, 256),
        ],
        compiler_params=pltpu.CompilerParams(vmem_limit_bytes=16 << 20),
        cost_estimate=pl.CostEstimate(flops=1_000_000, bytes_accessed=1_000, transcendentals=0),
        name="front",
    )(masks, *pieces, *prepared, *heads[:2])


def own_product(planes, row_h, row_l, col_h, col_l, *xs):
    def kernel(row_h, row_l, col_h, col_l, xa_h, xa_l, xb_h, xb_l, c_leaf):
        for j in range(2, xa_h.shape[0]):
            own_columns(j, row_h, row_l, col_h, col_l, (xa_h, xa_l, xb_h, xb_l), c_leaf, 2, planes)

    return pl.pallas_call(
        kernel,
        out_shape=jax.ShapeDtypeStruct((xs[0].shape[0] - 2, 512, 256), F32),
        in_specs=[VMEM] * 8,
        out_specs=VMEM,
        compiler_params=pltpu.CompilerParams(vmem_limit_bytes=12 << 20),
        cost_estimate=pl.CostEstimate(flops=1_000_000, bytes_accessed=1_000, transcendentals=0),
        name="own_product",
    )(row_h, row_l, col_h, col_l, *xs)


def make_back_kernel(planes, leaves):
    def kernel(
        mask_ref, b0, b1, b2, b3, xa_h, xa_l, ta_h, ta_l, tla_h, tla_l,
        xb_h, xb_l, tb_h, tb_l, tlb_h, tlb_l, base_top, base_leaf, c_top, c_leaf,
        col_top, diag_top, col_mid, cross_mid, diag_mid, col_leaf, cross_c, cross_e, diag_leaf,
        blocks, a_h, a_l, cb_h, cb_l, c_s, d_s, e_s, f_s, top_s, mid_s, sem,
    ):
        device = lax.axis_index("row")
        plane = own_plane(device, planes)
        quarter = device % 4
        half = device % 2
        copies = []

        def move(src, dst):
            copy = pltpu.make_async_copy(src, dst, sem.at[len(copies)])
            copy.start()
            copies.append(copy)
            return copy

        masks = [-mask_ref[r : r + 1, :] for r in range(4)]
        near = places(planes)[1] == 0
        for k, ref in enumerate((b0, b1, b2, b3)):
            for n in range(6):
                blocks[n, :, at((quarter ^ k) * 32, 32), :] = ref[:, n * 32 : n * 32 + 32, :]
        for n, (row, col) in enumerate(((1, 1), (1, 2), (1, 3), (2, 2), (3, 3), (3, 2))):
            re, im = blocks[n, 0], blocks[n, 1]
            put_pair(a_h, a_l, row * 128 - 128, col * 256 - 256, re, im)
            if row != col:
                put_pair(a_h, a_l, col * 128 - 128, row * 256 - 256, re.T, im.T)

        def columns(j, out):
            xh = jnp.concatenate([pick(near, r, xa_h, xb_h, j) for r in (1, 2, 3)], axis=0)
            xl = jnp.concatenate([pick(near, r, xa_l, xb_l, j) for r in (1, 2, 3)], axis=0)
            got = mm3(a_h[...], a_l[...], xh, xl)
            for r in range(4):
                rows = slice(r * 128, r * 128 + 128)
                place = at((plane ^ r) * 128, 128)
                for part in (0, 1):
                    lanes = slice(part * 128, part * 128 + 128)
                    c = c_leaf[j - 2, rows, lanes] if j > 1 else c_top[j, rows, lanes]
                    if r:
                        c = c + got[r * 128 - 128 : r * 128, lanes]
                    c = c * masks[r]
                    hi, lo = halves(c)
                    cb_h[j, rows, lanes] = hi
                    cb_l[j, rows, lanes] = lo
                    out[part, place, :] = c

        def against(j, t_h, t_l):
            got = mm3(t_h, t_l, cb_h[j], cb_l[j])
            outs = []
            for n in range(t_h.shape[0] // 256):
                g = got[n * 256 : n * 256 + 256]
                outs.append((g[0:128, 0:128] - g[128:256, 128:256], g[0:128, 128:256] + g[128:256, 0:128]))
            return outs

        def across(first, second):
            return jnp.concatenate([jnp.where(near, first, second), jnp.where(near, second, first)], axis=1)

        tt_h, tt_l = across(ta_h[...], tb_h[...]), across(ta_l[...], tb_l[...])

        def leaf_tail(j):
            th = jnp.concatenate([tt_h, across(tla_h[j], tlb_h[j])], axis=0)
            tl = jnp.concatenate([tt_l, across(tla_l[j], tlb_l[j])], axis=0)
            zs = against(2 + j, th, tl)
            for n, (z, out) in enumerate(zip(zs, (e_s, d_s, f_s))):
                for part in (0, 1):
                    out[j, part] = base_leaf[j, n, part] - z[part]
            mine = slice(j * 128, j * 128 + 128)
            move(e_s.at[j], cross_e.at[:, mine, :])
            move(d_s.at[j], cross_c.at[:, mine, :])
            move(f_s.at[j], diag_leaf.at[:, mine, :])

        for j in range(leaves):
            columns(2 + j, c_s.at[2 + j])
            move(c_s.at[2 + j], col_leaf.at[:, j * 512 : j * 512 + 512, :])
        columns(1, c_s.at[1])
        move(c_s.at[1, :, at(half * 256, 256), :], col_mid)
        columns(0, c_s.at[0])
        move(c_s.at[0, :, at(quarter * 128, 128), :], col_top)
        for j in range(leaves):
            leaf_tail(j)
        zs = against(1, tt_h, tt_l)
        for n in (0, 1):
            for part in (0, 1):
                mid_s[n, part] = base_top[1 + n, part] - zs[n][part]
        move(mid_s.at[0, :, at(half * 64, 64), :], cross_mid)
        move(mid_s.at[1, :, at(half * 64, 64), :], diag_mid)
        (z,) = against(0, tt_h[0:256], tt_l[0:256])
        for part in (0, 1):
            top_s[part] = base_top[0, part] - z[part]
        move(top_s.at[:, at(quarter * 32, 32), :], diag_top)
        for copy in copies:
            copy.wait()

    return kernel


def back(planes, masks, root, firsts, leaves):
    n = leaves + 2
    v = pltpu.VMEM
    shapes = [(2, 128, 128), (2, 32, 128), (2, 256, 128), (2, 64, 128), (2, 64, 128)]
    shapes += [(2, leaves * rows, 128) for rows in (512, 128, 128, 128)]
    pair = lambda *shape: [v(shape, BF16)] * 2
    return pl.pallas_call(
        make_back_kernel(planes, leaves),
        out_shape=tuple(jax.ShapeDtypeStruct(s, F32) for s in shapes),
        in_specs=[VMEM] * (5 + len(firsts)),
        out_specs=(ANY,) * len(shapes),
        scratch_shapes=[
            v((6, 2, 128, 128), F32), *pair(384, 768), *pair(n, 512, 256), v((n, 2, 512, 128), F32),
            v((leaves, 2, 128, 128), F32), v((leaves, 2, 128, 128), F32), v((leaves, 2, 128, 128), F32),
            v((2, 128, 128), F32), v((2, 2, 128, 128), F32),
            pltpu.SemaphoreType.DMA((10 + 4 * leaves,)),
        ],
        compiler_params=pltpu.CompilerParams(vmem_limit_bytes=24 << 20),
        cost_estimate=pl.CostEstimate(flops=8_000_000_000, bytes_accessed=12_000_000, transcendentals=0),
        name="back",
    )(masks, *root, *firsts)


def root_gathered(ainv_root):
    device = lax.axis_index("row")
    full = lax.all_gather(ainv_root, "row", axis=1, tiled=True)
    quarter = device % 4
    own = lax.dynamic_slice_in_dim(full, quarter * 32, 32, 1)
    root = []
    for k in range(4):
        pieces = []
        for row, col in ((1, 1), (1, 2), (1, 3), (2, 2), (3, 3), (3, 2)):
            block = full[:, row * 128 : row * 128 + 128, col * 128 : col * 128 + 128]
            pieces.append(lax.dynamic_slice_in_dim(block, (quarter ^ k) * 32, 32, 1))
        root.append(jnp.concatenate(pieces, axis=1))
    return own, root


def local(
    ainv_root, pattern, panel_top, inv_top, panel_mid, link_mid, inv_mid,
    panel_leaf, link_leaf_mid, link_leaf_top, inv_leaf,
):
    planes = lax.axis_size("row") == 16
    leaves = panel_leaf.shape[1] // 512
    prepared = prep(panel_leaf, link_leaf_mid, link_leaf_top, inv_leaf)
    if planes:
        top, mine, masks, *sent = pack(
            pattern, ainv_root, panel_top, inv_top, panel_mid, link_mid, inv_mid
        )
        got = [swap(x, 4 * k) for k, x in zip((1, 2, 3), sent)]
        other = swap(mine, 1)
        heads = head(planes, masks, mine, other, prepared)
        *got, _ = lax.optimization_barrier((*got, heads))
        lead, rest, both = join(*got, swap(top, 2))
        far = [swap(lead, 4), swap(rest, 2)]
    else:
        node = lax.dynamic_index_in_dim(pattern, lax.axis_index("row") // 4, 0, keepdims=False)
        masks = jnp.broadcast_to(jnp.pad(node.astype(F32), (0, 4))[:, None], (8, 128))
        own, root = root_gathered(ainv_root)
        own = [own[:, :, n * 128 : n * 128 + 128] for n in range(4)]
        top = jnp.concatenate([panel_top, inv_top, *own], axis=1)
        mine = jnp.concatenate([top, panel_mid, link_mid, inv_mid], axis=1)
        both = jnp.concatenate([root[0], swap(top, 2)], axis=1)
        other = swap(mine, 1)
        heads = head(planes, masks, mine, other, prepared)
    pieces = [mine, other, both, swap(both, 1)]
    firsts = front(planes, masks, pieces, prepared, heads)
    if planes:
        *far, firsts = lax.optimization_barrier((*far, firsts))
        far = stack(*far)
        root = [both, pieces[3], far, swap(far, 1)]
    c_leaf = own_product(planes, *firsts[8:12], *heads[:2], *firsts[:2])
    return back(planes, masks, root, [*heads, *firsts[:8], firsts[12], c_leaf], leaves)


def solution(mesh):
    split = P("pole", "row", None)
    return jax.shard_map(
        local,
        mesh=mesh,
        in_specs=(split, P()) + (split,) * 9,
        out_specs=(split,) * 9,
        check_vma=False,
    )
```

```python
import jax
import jax.numpy as jnp
from jax import lax
from jax.experimental import pallas as pl
from jax.experimental.pallas import tpu as pltpu
from jax.sharding import PartitionSpec as P

F32 = jnp.float32
BF16 = jnp.bfloat16
ANY = pl.BlockSpec(memory_space=pl.ANY)
VMEM = pl.BlockSpec(memory_space=pltpu.VMEM)


def swap(x, apart):
    return lax.ppermute(x, "row", [(i, i ^ apart) for i in range(lax.axis_size("row"))])


def halves(x):
    hi = x.astype(BF16)
    return hi, (x - hi.astype(F32)).astype(BF16)


def mm(a, b):
    return jnp.dot(a, b, preferred_element_type=F32)


def mm3(ah, al, bh, bl):
    left = jnp.concatenate([ah, ah, al], axis=1)
    return mm(left, jnp.concatenate([bh, bl, bh], axis=0))


def at(start, size):
    return pl.ds(pl.multiple_of(start, size), size)


def in_hbm(x):
    return pltpu.with_memory_space_constraint(x, pltpu.HBM)


def own_plane(device, planes):
    return device // 4 if planes else device * 0


def pack_kernel(
    pat, a_hbm, t_hbm, i_hbm, pm_hbm, lm_hbm, im_hbm, top, mine, masks, z1, z2, z3, a, pat_s, sem
):
    plane = lax.axis_index("row") // 4
    pairs = (
        (a_hbm, a), (t_hbm, mine.at[:, 0:128, :]), (i_hbm, mine.at[:, 128:160, :]), (pat, pat_s),
        (pm_hbm, mine.at[:, 288:544, :]), (lm_hbm, mine.at[:, 544:608, :]), (im_hbm, mine.at[:, 608:672, :]),
    )
    copies = [pltpu.make_async_copy(src, dst, sem.at[n]) for n, (src, dst) in enumerate(pairs)]
    for copy in copies:
        copy.start()
    copies[0].wait()
    for dst in (top, mine):
        for n in range(4):
            dst[:, 160 + n * 32 : 192 + n * 32, :] = a[:, :, n * 128 : n * 128 + 128]
    for dst, order in ((z1, (0, 3, 2)), (z2, (0,)), (z3, (0, 1))):
        for n, apart in enumerate(order):
            dst[:, n * 32 : n * 32 + 32, :] = a[:, :, at((plane ^ apart) * 128, 128)]
    copies[1].wait()
    copies[2].wait()
    top[:, 0:160, :] = mine[:, 0:160, :]
    copies[3].wait()
    for r in range(4):
        masks[r : r + 1, :] = jnp.full((1, 128), pat_s[plane, plane ^ r], jnp.int32).astype(F32)
    masks[4:8, :] = jnp.zeros((4, 128), F32)
    for copy in copies[4:]:
        copy.wait()


def pack(pattern, *mine):
    shapes = [(2, 288, 128), (2, 672, 128), (8, 128), (2, 96, 128), (2, 32, 128), (2, 64, 128)]
    return pl.pallas_call(
        pack_kernel,
        out_shape=tuple(jax.ShapeDtypeStruct(s, F32) for s in shapes),
        in_specs=[ANY] * 7,
        out_specs=(VMEM,) * len(shapes),
        scratch_shapes=[
            pltpu.VMEM(mine[0].shape, F32), pltpu.SMEM(pattern.shape, jnp.int32), pltpu.SemaphoreType.DMA((7,)),
        ],
        compiler_params=pltpu.CompilerParams(vmem_limit_bytes=4 << 20),
        cost_estimate=pl.CostEstimate(flops=1_000_000, bytes_accessed=1_000, transcendentals=0),
        name="pack_panels",
    )(in_hbm(pattern), *(in_hbm(x) for x in mine))


def join_kernel(z1, z2, z3, far_top, lead, rest, both):
    plane = lax.axis_index("row") // 4
    for n, apart in enumerate((0, 3, 2)):
        lead[:, n * 32 : n * 32 + 32, :] = far_top[:, at(160 + (plane ^ apart) * 32, 32), :]
    rest[:, 0:32, :] = z2[...]
    rest[:, 32:96, :] = z3[...]
    both[:, 0:96, :] = z1[...]
    both[:, 96:128, :] = z2[...]
    both[:, 128:192, :] = z3[...]
    both[:, 192:480, :] = far_top[...]


def join(*blocks):
    return pl.pallas_call(
        join_kernel,
        out_shape=tuple(jax.ShapeDtypeStruct((2, rows, 128), F32) for rows in (96, 96, 480)),
        in_specs=[VMEM] * 4,
        out_specs=(VMEM,) * 3,
        compiler_params=pltpu.CompilerParams(vmem_limit_bytes=4 << 20),
        cost_estimate=pl.CostEstimate(flops=1_000_000, bytes_accessed=1_000, transcendentals=0),
        name="join_root",
    )(*blocks)


def stack_kernel(upper, lower, joined):
    joined[:, 0:96, :] = upper[...]
    joined[:, 96:192, :] = lower[...]


def stack(upper, lower):
    return pl.pallas_call(
        stack_kernel,
        out_shape=jax.ShapeDtypeStruct((2, 192, 128), F32),
        in_specs=[VMEM] * 2,
        out_specs=VMEM,
        compiler_params=pltpu.CompilerParams(vmem_limit_bytes=4 << 20),
        cost_estimate=pl.CostEstimate(flops=1_000_000, bytes_accessed=1_000, transcendentals=0),
        name="stack_root",
    )(upper, lower)


def put_rhs(ref_h, ref_l, row, re, im):
    rh, rl = halves(re)
    ih, il = halves(im)
    for ref, r, i in ((ref_h, rh, ih), (ref_l, rl, il)):
        ref[row : row + 128, 0:128] = r
        ref[row : row + 128, 128:256] = i
        ref[row + 128 : row + 256, 0:128] = -i
        ref[row + 128 : row + 256, 128:256] = r


def put_pair(ref_h, ref_l, row, col, re, im):
    n = re.shape[0]
    rh, rl = halves(re)
    ih, il = halves(im)
    for ref, r, i in ((ref_h, rh, ih), (ref_l, rl, il)):
        ref[row : row + n, col : col + 128] = r
        ref[row : row + n, col + 128 : col + 256] = i


def put_transposed(ref_h, ref_l, row, r, re, im):
    for part, x in ((0, re), (128, im)):
        xh, xl = halves(x.T)
        ref_h[row + part : row + part + 128, r * 128 : r * 128 + 128] = xh
        ref_l[row + part : row + part + 128, r * 128 : r * 128 + 128] = xl


def make_prep_kernel(leaves):
    def kernel(panel, link_c, link_e, inv, g, li, rhs_h, rhs_l, auxl_h, auxl_l, lc_s, le_s, sem):
        pairs = ((link_c, lc_s), (link_e, le_s), (panel, g), (inv, li))
        copies = [pltpu.make_async_copy(src, dst, sem.at[n]) for n, (src, dst) in enumerate(pairs)]
        for copy in copies:
            copy.start()
        for row, ref, copy in ((0, lc_s, copies[0]), (256, le_s, copies[1])):
            copy.wait()
            for j in range(leaves):
                mine = slice(j * 128, j * 128 + 128)
                re, im = ref[0, mine], ref[1, mine]
                put_rhs(rhs_h.at[j], rhs_l.at[j], row, re, im)
                put_pair(auxl_h.at[j], auxl_l.at[j], 0, row, re.T, im.T)
        copies[2].wait()
        copies[3].wait()

    return kernel


def prep(panel, link_c, link_e, inv):
    leaves = panel.shape[1] // 512
    v = pltpu.VMEM
    out = [(panel.shape, F32), (inv.shape, F32)]
    out += [((leaves, 512, 256), BF16)] * 2 + [((leaves, 128, 512), BF16)] * 2
    return pl.pallas_call(
        make_prep_kernel(leaves),
        out_shape=tuple(jax.ShapeDtypeStruct(s, d) for s, d in out),
        in_specs=[ANY] * 4,
        out_specs=(VMEM,) * len(out),
        scratch_shapes=[v(link_c.shape, F32), v(link_e.shape, F32), pltpu.SemaphoreType.DMA((4,))],
        compiler_params=pltpu.CompilerParams(vmem_limit_bytes=12 << 20),
        cost_estimate=pl.CostEstimate(flops=1_000_000, bytes_accessed=1_000, transcendentals=0),
        name="prep",
    )(in_hbm(panel), in_hbm(link_c), in_hbm(link_e), in_hbm(inv))


def put_block(x_h, x_l, t_h, t_l, row, e, re, im):
    put_rhs(x_h, x_l, e * 256, re, im)
    put_transposed(t_h, t_l, row, e, re, im)


def places(planes):
    device = lax.axis_index("row")
    plane = own_plane(device, planes)
    shift = plane ^ (device % 4)
    return plane, shift // 2, shift % 2 == 1


def mid_blocks(planes, mine, other, b_s, am_s, ra_h, ra_l):
    plane = places(planes)[0]
    half = lax.axis_index("row") % 2
    for k, ref in enumerate((mine, other)):
        h = half ^ k
        for n in (0, 1):
            place = at(((h * 2 + n) ^ plane) * 128, 128)
            b_s[:, place, :] = ref[:, 288 + n * 128 : 416 + n * 128, :]
        am_s[:, at(h * 64, 64), :] = ref[:, 544:608, :]
    put_rhs(ra_h, ra_l, 0, am_s[0], am_s[1])


def top_block(e, swapped, first, second, row, mask):
    left, right = (second, first) if e == 0 else (first, second)
    return tuple(
        jnp.where(swapped, left[part, row : row + 128], right[part, row : row + 128]) * mask for part in (0, 1)
    )


def mid_block(block, mask, b_s, got):
    rows = at(block * 128, 128)
    return tuple(b_s[part, rows] * mask - got[:, part * 128 : part * 128 + 128] for part in (0, 1))


def leaf_block(j, supernode, mask, g, got):
    rows = at(j * 512 + supernode * 128, 128)
    return tuple(g[part, rows] * mask - got[:, part * 128 : part * 128 + 128] for part in (0, 1))


def make_head_kernel(planes):
    def kernel(
        mask_ref, mine, other, g, rhs_h, rhs_l, x_h, x_l, t_h, t_l, tl_h, tl_l, b_s, ra_h, ra_l, at_h, at_l,
        am_s, lhs_h, lhs_l,
    ):
        plane, pair, swapped = places(planes)
        mid_blocks(planes, mine, other, b_s, am_s, ra_h, ra_l)
        put_pair(at_h, at_l, 0, 0, am_s[0].T, am_s[1].T)
        masks = [mask_ref[pl.ds(pair * 2 + e, 1), :] for e in (0, 1)]
        for e in (0, 1):
            re, im = top_block(e, swapped, mine, other, 0, masks[e])
            put_pair(lhs_h, lhs_l, e * 128, 256, re, im)
            put_block(x_h.at[0], x_l.at[0], t_h, t_l, 0, e, re, im)
        got = mm3(lhs_h[:, 256:512], lhs_l[:, 256:512], ra_h[...], ra_l[...])
        for e in (0, 1):
            re, im = mid_block(pair * 2 + e, masks[e], b_s, got[e * 128 : e * 128 + 128])
            put_pair(lhs_h, lhs_l, e * 128, 0, re, im)
            put_block(x_h.at[1], x_l.at[1], t_h, t_l, 256, e, re, im)
        for j in range(x_h.shape[0] - 2):
            got = mm3(lhs_h[...], lhs_l[...], rhs_h[j], rhs_l[j])
            for e in (0, 1):
                supernode = plane ^ (pair * 2 + e)
                re, im = leaf_block(j, supernode, masks[e], g, got[e * 128 : e * 128 + 128])
                put_block(x_h.at[2 + j], x_l.at[2 + j], tl_h.at[j], tl_l.at[j], 0, e, re, im)

    return kernel


def head(planes, masks, mine, other, prepared):
    g, _, rhs_h, rhs_l, _, _ = prepared
    leaves = g.shape[1] // 512
    v = pltpu.VMEM
    pair = lambda *shape: [v(shape, BF16)] * 2
    shapes = [(leaves + 2, 512, 256)] * 2 + [(512, 256)] * 2 + [(leaves, 256, 256)] * 2
    shapes += [(2, 512, 128), (256, 256), (256, 256), (128, 256), (128, 256)]
    return pl.pallas_call(
        make_head_kernel(planes),
        out_shape=tuple(jax.ShapeDtypeStruct(s, BF16 if len(s) != 3 or s[0] != 2 else F32) for s in shapes),
        in_specs=[VMEM] * 6,
        out_specs=(VMEM,) * len(shapes),
        scratch_shapes=[v((2, 128, 128), F32), *pair(256, 512)],
        compiler_params=pltpu.CompilerParams(vmem_limit_bytes=16 << 20),
        cost_estimate=pl.CostEstimate(flops=1_000_000, bytes_accessed=1_000, transcendentals=0),
        name="head",
    )(masks, mine, other, g, rhs_h, rhs_l)


def pick(near, r, first, second, j):
    rows = slice(r % 2 * 256, r % 2 * 256 + 256)
    if r < 2:
        return jnp.where(near, first[j, rows], second[j, rows])
    return jnp.where(near, second[j, rows], first[j, rows])


def own_columns(j, row_h, row_l, col_h, col_l, xs, out, first, planes):
    near = places(planes)[1] == 0
    xa_h, xa_l, xb_h, xb_l = xs
    xh = jnp.concatenate([xa_h[j], xb_h[j]], axis=0)
    xl = jnp.concatenate([xa_l[j], xb_l[j]], axis=0)
    out[j - first, 0:128] = mm3(row_h[...], row_l[...], xh, xl)
    out[j - first, 128:512] = mm3(
        col_h[...], col_l[...], pick(near, 0, xa_h, xb_h, j), pick(near, 0, xa_l, xb_l, j)
    )


def make_front_kernel(planes, leaves):
    def kernel(
        mask_ref, mine, other, both, both_other, g_s, li_s, rhs_h, rhs_l, auxl_h, auxl_l, xa_h, xa_l,
        b_s, ra_h, ra_l, aux_h, aux_l, x_h, x_l, t_h, t_l, tl_h, tl_l, base_top, base_leaf, row_h, row_l, col_h, col_l, c_top,
        t0_s, d_s, own, lhs_h, lhs_l, rq_h, rq_l, rrs_h, rrs_l,
    ):
        device = lax.axis_index("row")
        plane = own_plane(device, planes)
        quarter = device % 4
        half = device % 2
        for k, (ref, row) in enumerate(((mine, 0), (other, 0), (both, 192), (both_other, 192))):
            q = quarter ^ k
            t0_s[:, at(q * 32, 32), :] = ref[:, row + 128 : row + 160, :]
            for n in range(4):
                own[:, at(q * 32, 32), n * 128 : n * 128 + 128] = (
                    ref[:, row + 160 + n * 32 : row + 192 + n * 32, :]
                )
        for k, ref in enumerate((mine, other)):
            d_s[:, at((half ^ k) * 64, 64), :] = ref[:, 608:672, :]
        _, pair, swapped = places(planes)
        pair = 1 - pair
        masks = [mask_ref[pl.ds(pair * 2 + e, 1), :] for e in (0, 1)]
        for e in (0, 1):
            re, im = top_block(e, swapped, both, both_other, 192, masks[e])
            put_pair(lhs_h, lhs_l, e * 128, 256, re, im)
            put_block(x_h.at[0], x_l.at[0], t_h, t_l, 0, e, re, im)
        put_pair(lhs_h, lhs_l, 384, 256, t0_s[0], t0_s[1])
        ah, al = ra_h[...], ra_l[...]
        got = mm3(lhs_h[0:256, 256:512], lhs_l[0:256, 256:512], ah, al)
        for e in (0, 1):
            re, im = mid_block(pair * 2 + e, masks[e], b_s, got[e * 128 : e * 128 + 128])
            put_pair(lhs_h, lhs_l, e * 128, 0, re, im)
            put_block(x_h.at[1], x_l.at[1], t_h, t_l, 256, e, re, im)
        got = mm3(lhs_h[384:512, 256:512], lhs_l[384:512, 256:512], ah, al)
        q_r, q_i = -got[:, 0:128], -got[:, 128:256]
        put_pair(lhs_h, lhs_l, 384, 0, q_r, q_i)
        put_pair(lhs_h, lhs_l, 256, 256, q_r.T, q_i.T)
        put_rhs(rq_h, rq_l, 0, q_r, q_i)
        got = mm3(aux_h[...], aux_l[...], rq_h[...], rq_l[...])
        d_r, d_i = d_s[0] - got[:, 0:128], d_s[1] - got[:, 128:256]
        put_pair(lhs_h, lhs_l, 256, 0, d_r, d_i)
        base_top[0] = t0_s[...]
        base_top[1, 0] = q_r
        base_top[1, 1] = q_i
        base_top[2, 0] = d_r
        base_top[2, 1] = d_i
        for n in range(4):
            cols = at((plane ^ (2 - pair * 2) ^ n) * 128, 128)
            put_pair(row_h, row_l, 0, n * 256, own[0, :, cols], own[1, :, cols])
        for r in range(1, 4):
            cols = at((plane ^ r) * 128, 128)
            put_pair(col_h, col_l, (r - 1) * 128, 0, own[0, :, cols].T, own[1, :, cols].T)
        for j in (0, 1):
            own_columns(j, row_h, row_l, col_h, col_l, (xa_h, xa_l, x_h, x_l), c_top, 0, planes)
        for j in range(leaves):
            got = mm3(lhs_h[...], lhs_l[...], rhs_h[j], rhs_l[j])
            for e in (0, 1):
                re, im = leaf_block(j, plane ^ (pair * 2 + e), masks[e], g_s, got[e * 128 : e * 128 + 128])
                put_block(x_h.at[2 + j], x_l.at[2 + j], tl_h.at[j], tl_l.at[j], 0, e, re, im)
            r_r, r_i = -got[256:384, 0:128], -got[256:384, 128:256]
            s_r, s_i = -got[384:512, 0:128], -got[384:512, 128:256]
            put_rhs(rrs_h.at[j], rrs_l.at[j], 0, r_r, r_i)
            put_rhs(rrs_h.at[j], rrs_l.at[j], 256, s_r, s_i)
            base_leaf[j, 0, 0] = s_r
            base_leaf[j, 0, 1] = s_i
            base_leaf[j, 1, 0] = r_r
            base_leaf[j, 1, 1] = r_i
        for j in range(leaves):
            mine_rows = slice(j * 128, j * 128 + 128)
            got = mm3(auxl_h[j], auxl_l[j], rrs_h[j], rrs_l[j])
            base_leaf[j, 2, 0] = li_s[0, mine_rows] - got[:, 0:128]
            base_leaf[j, 2, 1] = li_s[1, mine_rows] - got[:, 128:256]

    return kernel


def front(planes, masks, pieces, prepared, heads):
    leaves = prepared[0].shape[1] // 512
    n = leaves + 2
    v = pltpu.VMEM
    out = [
        ((n, 512, 256), BF16), ((n, 512, 256), BF16), ((512, 256), BF16), ((512, 256), BF16),
        ((leaves, 256, 256), BF16), ((leaves, 256, 256), BF16),
        ((3, 2, 128, 128), F32), ((leaves, 3, 2, 128, 128), F32),
        ((128, 1024), BF16), ((128, 1024), BF16), ((384, 256), BF16), ((384, 256), BF16),
        ((2, 512, 256), F32),
    ]
    pair = lambda *shape: [v(shape, BF16)] * 2
    return pl.pallas_call(
        make_front_kernel(planes, leaves),
        out_shape=tuple(jax.ShapeDtypeStruct(s, d) for s, d in out),
        in_specs=[VMEM] * 18,
        out_specs=(VMEM,) * len(out),
        scratch_shapes=[
            v((2, 128, 128), F32), v((2, 128, 128), F32),
            v((2, 128, 512), F32), *pair(512, 512), *pair(256, 256),
            *pair(leaves, 512, 256),
        ],
        compiler_params=pltpu.CompilerParams(vmem_limit_bytes=16 << 20),
        cost_estimate=pl.CostEstimate(flops=1_000_000, bytes_accessed=1_000, transcendentals=0),
        name="front",
    )(masks, *pieces, *prepared, *heads[:2], *heads[6:])


def own_product(planes, row_h, row_l, col_h, col_l, *xs):
    def kernel(row_h, row_l, col_h, col_l, xa_h, xa_l, xb_h, xb_l, c_leaf):
        for j in range(2, xa_h.shape[0]):
            own_columns(j, row_h, row_l, col_h, col_l, (xa_h, xa_l, xb_h, xb_l), c_leaf, 2, planes)

    return pl.pallas_call(
        kernel,
        out_shape=jax.ShapeDtypeStruct((xs[0].shape[0] - 2, 512, 256), F32),
        in_specs=[VMEM] * 8,
        out_specs=VMEM,
        compiler_params=pltpu.CompilerParams(vmem_limit_bytes=12 << 20),
        cost_estimate=pl.CostEstimate(flops=1_000_000, bytes_accessed=1_000, transcendentals=0),
        name="own_product",
    )(row_h, row_l, col_h, col_l, *xs)


def make_back_kernel(planes, leaves):
    def kernel(
        mask_ref, b0, b1, b2, b3, xa_h, xa_l, ta_h, ta_l, tla_h, tla_l,
        xb_h, xb_l, tb_h, tb_l, tlb_h, tlb_l, base_top, base_leaf, c_top, c_leaf,
        col_top, diag_top, col_mid, cross_mid, diag_mid, col_leaf, cross_c, cross_e, diag_leaf,
        blocks, a_h, a_l, cb_h, cb_l, c_s, d_s, e_s, f_s, top_s, mid_s, sem,
    ):
        device = lax.axis_index("row")
        plane = own_plane(device, planes)
        quarter = device % 4
        half = device % 2
        copies = []

        def move(src, dst):
            copy = pltpu.make_async_copy(src, dst, sem.at[len(copies)])
            copy.start()
            copies.append(copy)
            return copy

        masks = [-mask_ref[r : r + 1, :] for r in range(4)]
        near = places(planes)[1] == 0
        for k, ref in enumerate((b0, b1, b2, b3)):
            for n in range(6):
                blocks[n, :, at((quarter ^ k) * 32, 32), :] = ref[:, n * 32 : n * 32 + 32, :]
        held = {}
        for n, (row, col) in enumerate(((1, 1), (1, 2), (1, 3), (2, 2), (3, 3), (3, 2))):
            re, im = blocks[n, 0], blocks[n, 1]
            held[row, col] = (re, im)
            if row != col:
                held[col, row] = (re.T, im.T)
        for row in (1, 2, 3):
            one, three = held[row, 1], held[row, 3]
            first = [jnp.where(near, x, y) for x, y in zip(one, three)]
            second = [jnp.where(near, y, x) for x, y in zip(one, three)]
            for place, (re, im) in enumerate((first, second, held[row, 2])):
                put_pair(a_h, a_l, row * 128 - 128, place * 256, re, im)

        def columns(j, out):
            xh = jnp.concatenate([xa_h[j, 256:512], xb_h[j, 256:512], pick(near, 2, xa_h, xb_h, j)], axis=0)
            xl = jnp.concatenate([xa_l[j, 256:512], xb_l[j, 256:512], pick(near, 2, xa_l, xb_l, j)], axis=0)
            got = mm3(a_h[...], a_l[...], xh, xl)
            for r in range(4):
                rows = slice(r * 128, r * 128 + 128)
                place = at((plane ^ r) * 128, 128)
                for part in (0, 1):
                    lanes = slice(part * 128, part * 128 + 128)
                    c = c_leaf[j - 2, rows, lanes] if j > 1 else c_top[j, rows, lanes]
                    if r:
                        c = c + got[r * 128 - 128 : r * 128, lanes]
                    c = c * masks[r]
                    hi, lo = halves(c)
                    cb_h[j, rows, lanes] = hi
                    cb_l[j, rows, lanes] = lo
                    out[part, place, :] = c

        def against(j, t_h, t_l):
            got = mm3(t_h, t_l, cb_h[j], cb_l[j])
            outs = []
            for n in range(t_h.shape[0] // 256):
                g = got[n * 256 : n * 256 + 256]
                outs.append((g[0:128, 0:128] - g[128:256, 128:256], g[0:128, 128:256] + g[128:256, 0:128]))
            return outs

        def across(first, second):
            return jnp.concatenate([jnp.where(near, first, second), jnp.where(near, second, first)], axis=1)

        tt_h, tt_l = across(ta_h[...], tb_h[...]), across(ta_l[...], tb_l[...])

        def leaf_tail(j):
            th = jnp.concatenate([tt_h, across(tla_h[j], tlb_h[j])], axis=0)
            tl = jnp.concatenate([tt_l, across(tla_l[j], tlb_l[j])], axis=0)
            zs = against(2 + j, th, tl)
            for n, (z, out) in enumerate(zip(zs, (e_s, d_s, f_s))):
                for part in (0, 1):
                    out[j, part] = base_leaf[j, n, part] - z[part]
            mine = slice(j * 128, j * 128 + 128)
            move(e_s.at[j], cross_e.at[:, mine, :])
            move(d_s.at[j], cross_c.at[:, mine, :])
            move(f_s.at[j], diag_leaf.at[:, mine, :])

        for j in range(leaves):
            columns(2 + j, c_s.at[2 + j])
            move(c_s.at[2 + j], col_leaf.at[:, j * 512 : j * 512 + 512, :])
        columns(1, c_s.at[1])
        move(c_s.at[1, :, at(half * 256, 256), :], col_mid)
        columns(0, c_s.at[0])
        move(c_s.at[0, :, at(quarter * 128, 128), :], col_top)
        for j in range(leaves):
            leaf_tail(j)
        zs = against(1, tt_h, tt_l)
        for n in (0, 1):
            for part in (0, 1):
                mid_s[n, part] = base_top[1 + n, part] - zs[n][part]
        move(mid_s.at[0, :, at(half * 64, 64), :], cross_mid)
        move(mid_s.at[1, :, at(half * 64, 64), :], diag_mid)
        (z,) = against(0, tt_h[0:256], tt_l[0:256])
        for part in (0, 1):
            top_s[part] = base_top[0, part] - z[part]
        move(top_s.at[:, at(quarter * 32, 32), :], diag_top)
        for copy in copies:
            copy.wait()

    return kernel


def back(planes, masks, root, firsts, leaves):
    n = leaves + 2
    v = pltpu.VMEM
    shapes = [(2, 128, 128), (2, 32, 128), (2, 256, 128), (2, 64, 128), (2, 64, 128)]
    shapes += [(2, leaves * rows, 128) for rows in (512, 128, 128, 128)]
    pair = lambda *shape: [v(shape, BF16)] * 2
    return pl.pallas_call(
        make_back_kernel(planes, leaves),
        out_shape=tuple(jax.ShapeDtypeStruct(s, F32) for s in shapes),
        in_specs=[VMEM] * (5 + len(firsts)),
        out_specs=(ANY,) * len(shapes),
        scratch_shapes=[
            v((6, 2, 128, 128), F32), *pair(384, 768), *pair(n, 512, 256), v((n, 2, 512, 128), F32),
            v((leaves, 2, 128, 128), F32), v((leaves, 2, 128, 128), F32), v((leaves, 2, 128, 128), F32),
            v((2, 128, 128), F32), v((2, 2, 128, 128), F32),
            pltpu.SemaphoreType.DMA((10 + 4 * leaves,)),
        ],
        compiler_params=pltpu.CompilerParams(vmem_limit_bytes=24 << 20),
        cost_estimate=pl.CostEstimate(flops=8_000_000_000, bytes_accessed=12_000_000, transcendentals=0),
        name="back",
    )(masks, *root, *firsts)


def root_gathered(ainv_root):
    device = lax.axis_index("row")
    full = lax.all_gather(ainv_root, "row", axis=1, tiled=True)
    quarter = device % 4
    own = lax.dynamic_slice_in_dim(full, quarter * 32, 32, 1)
    root = []
    for k in range(4):
        pieces = []
        for row, col in ((1, 1), (1, 2), (1, 3), (2, 2), (3, 3), (3, 2)):
            block = full[:, row * 128 : row * 128 + 128, col * 128 : col * 128 + 128]
            pieces.append(lax.dynamic_slice_in_dim(block, (quarter ^ k) * 32, 32, 1))
        root.append(jnp.concatenate(pieces, axis=1))
    return own, root


def local(
    ainv_root, pattern, panel_top, inv_top, panel_mid, link_mid, inv_mid,
    panel_leaf, link_leaf_mid, link_leaf_top, inv_leaf,
):
    planes = lax.axis_size("row") == 16
    leaves = panel_leaf.shape[1] // 512
    prepared = prep(panel_leaf, link_leaf_mid, link_leaf_top, inv_leaf)
    if planes:
        top, mine, masks, *sent = pack(
            pattern, ainv_root, panel_top, inv_top, panel_mid, link_mid, inv_mid
        )
        got = [swap(x, 4 * k) for k, x in zip((1, 2, 3), sent)]
        other = swap(mine, 1)
        heads = head(planes, masks, mine, other, prepared)
        *got, _ = lax.optimization_barrier((*got, heads))
        lead, rest, both = join(*got, swap(top, 2))
        far = [swap(lead, 4), swap(rest, 2)]
    else:
        node = lax.dynamic_index_in_dim(pattern, lax.axis_index("row") // 4, 0, keepdims=False)
        masks = jnp.broadcast_to(jnp.pad(node.astype(F32), (0, 4))[:, None], (8, 128))
        own, root = root_gathered(ainv_root)
        own = [own[:, :, n * 128 : n * 128 + 128] for n in range(4)]
        top = jnp.concatenate([panel_top, inv_top, *own], axis=1)
        mine = jnp.concatenate([top, panel_mid, link_mid, inv_mid], axis=1)
        both = jnp.concatenate([root[0], swap(top, 2)], axis=1)
        other = swap(mine, 1)
        heads = head(planes, masks, mine, other, prepared)
    pieces = [mine, other, both, swap(both, 1)]
    firsts = front(planes, masks, pieces, prepared, heads)
    if planes:
        *far, firsts = lax.optimization_barrier((*far, firsts))
        far = stack(*far)
        root = [both, pieces[3], far, swap(far, 1)]
    c_leaf = own_product(planes, *firsts[8:12], *heads[:2], *firsts[:2])
    return back(planes, masks, root, [*heads[:6], *firsts[:8], firsts[12], c_leaf], leaves)


def solution(mesh):
    split = P("pole", "row", None)
    return jax.shard_map(
        local,
        mesh=mesh,
        in_specs=(split, P()) + (split,) * 9,
        out_specs=(split,) * 9,
        check_vma=False,
    )
```
